128 devices in a mesh: tm: 8 (over x, core), chan: 16 (over z, y).
Axes of the slice: x: 4, y: 4, z: 4, core: 2. Of those that a mesh axis runs over, the one named last changes fastest.
Arguments:
- raw_data: float32 [1024, 5120], P('chan', 'tm'), may hold values from -400 to 400
- whiten_taps: float32 [1024, 16], P('chan'), may hold values from -0.6 to 0.6
- band_taps: bfloat16 [113], replicated, may hold values from -0.5 to 0.5
- templates: bfloat16 [512, 512], P('tm'), may hold values from -5 to 5
- channel_mask: int32 [512, 1024], P('tm', 'chan'), may hold values 0 or 1
- moveouts: int32 [1024], P('chan'), may hold values from 0 to 511, as said below
Outputs:
- stacked: float32 [4096, 512], P('chan', 'tm')
The draws below stay inside these ranges and needn't reach their ends.
Inputs may be any that keep to these rules, and one draw needn't show every extreme that they name: `moveouts`: a channel's moveout; 0 on some channel and 511 on some channel.
All inputs are finite; a program needn't handle non-finite values. No bound on the sum of `channel_mask` on one device may be relied on, other than what follows from the above.
Results may differ from the reference program's by a relative error of at most 0.0041.
Values may be sent and summed in bfloat16 or wider, within the bound.
No kernel may reach another device: no remote copies, remote signals or barrier semaphores. Data moves between devices by JAX's collectives and lax.ppermute only.
A program may use at most 128 MiB of HBM per device.

```python
import math
import jax
import jax.numpy as jnp
from jax import lax

K = 512
L = 512
SPAN = 512
FW = 16
FB = 113
CH = 1024
NOUT = 4096
TIME = 5120


def draw_raw_data(key, part):
    key = jax.random.fold_in(key, 11)
    noise_key, chan_key, env_key = jax.random.split(key, 3)
    chan_scale = jnp.exp(math.log(10.0) * jax.random.uniform(chan_key, (CH, 1), jnp.float32))
    envelope = jnp.exp(math.log(10.0) * jax.random.uniform(env_key, (CH, TIME // 16 + 1), jnp.float32))
    envelope = jnp.repeat(envelope, 16, axis=1)[:, :TIME]
    values = jnp.clip(jax.random.normal(noise_key, (CH, TIME), jnp.float32), -4.0, 4.0)
    return (values * chan_scale * envelope).astype(jnp.float32)


def draw_moveouts(key, part):
    key = jax.random.fold_in(key, 23)
    base_key, first_key, second_key = jax.random.split(key, 3)
    moveout = jax.random.randint(base_key, (CH,), 0, SPAN)
    low_pos = jax.random.randint(first_key, (), 0, CH)
    high_pos = (low_pos + jax.random.randint(second_key, (), 1, CH)) % CH
    return moveout.at[low_pos].set(0).at[high_pos].set(SPAN - 1).astype(jnp.int32)


def plant(drawn, key, low, largest):
    index_at = [jax.random.randint(jax.random.fold_in(key, axis), (), 0, length) for axis, length in enumerate(drawn.shape)]
    widest = drawn.shape.index(max(drawn.shape))
    beside = index_at[:widest] + [(index_at[widest] + 1) % drawn.shape[widest]] + index_at[widest + 1:]
    return drawn.at[tuple(index_at)].set(low).at[tuple(beside)].set(largest)


def shard_levels(stream_key, dims, cuts, least, high):
    def one(position, blocks):
        heights = jax.random.uniform(jax.random.fold_in(jax.random.fold_in(stream_key, 6), position), (blocks,), jnp.float32, least / len(cuts), high / len(cuts))
        return jnp.repeat(jnp.exp(heights), dims[position] // blocks).reshape((-1,) + (1,) * (len(dims) - position - 1))

    gain = one(*cuts[0])
    for cut in cuts[1:]:
        gain = gain * one(*cut)
    return gain


def bell_draw(stream_key, shape, width, reach, pieces=(), kind=jnp.bfloat16):
    loudness = shard_levels(stream_key, shape, pieces, -0.22, 0.18) if pieces else 1.0
    entries = jax.random.normal(stream_key, shape, jnp.float32) * width * loudness
    return jnp.minimum(jnp.maximum(entries, -reach), reach).astype(kind)


def setup_inputs(seed: int = 0) -> dict:
    seeds = jax.random.split(jax.random.key(seed), 7)
    return {
        "raw_data": draw_raw_data(jax.random.fold_in(seeds[6], 71), 0),
        "whiten_taps": bell_draw(seeds[1], (CH, FW), 0.15, 0.6, ((0, 16),), jnp.float32),
        "band_taps": bell_draw(seeds[2], (FB,), FB ** -0.5, 0.5),
        "templates": bell_draw(seeds[3], (K, L), 1.0, 5.0, ((0, 8),)),
        "channel_mask": plant((jax.random.randint(seeds[4], (K, CH), 0, 2) < 1).astype(jnp.int32), jax.random.fold_in(seeds[4], 1), 0, 1),
        "moveouts": draw_moveouts(jax.random.fold_in(seeds[6], 71), 0),
    }


EPSILON = 1e-06

def reference(raw_data, whiten_taps, band_taps, templates, channel_mask, moveouts):
    padded = jnp.pad(raw_data, ((0, 0), (FW, 0)))
    whitened = raw_data
    for lag_step in range(1, FW + 1):
        whitened = whitened - whiten_taps[:, lag_step - 1:lag_step] * padded[:, FW - lag_step:FW - lag_step + TIME]
    whitened = lax.optimization_barrier(whitened.astype(jnp.bfloat16)).astype(jnp.float32)
    shifted = jnp.pad(whitened, ((0, 0), (FB - 1, 0)))
    band_float = band_taps.astype(jnp.float32)
    filtered = jnp.zeros(raw_data.shape, jnp.float32)
    for tap_index in range(FB):
        filtered = filtered + band_float[tap_index] * shifted[:, FB - 1 - tap_index:FB - 1 - tap_index + TIME]
    filtered = filtered.astype(jnp.bfloat16)
    aligned_len = NOUT + L - 1
    aligned = jax.vmap(lambda series, moveout: lax.dynamic_slice_in_dim(series, moveout.astype(jnp.int32), aligned_len))(filtered, moveouts)
    squares = jnp.square(aligned.astype(jnp.float32))
    running = jnp.concatenate([jnp.zeros((CH, 1), jnp.float32), jnp.cumsum(squares, axis=1)], axis=1)
    energy = running[:, L:L + NOUT] - running[:, :NOUT]
    data_scale = 1.0 / jnp.sqrt(energy / L + EPSILON)
    tmpl_float = templates.astype(jnp.float32)
    template_scale = 1.0 / (L * jnp.sqrt(lax.optimization_barrier(jnp.mean(tmpl_float * tmpl_float, axis=1)) + EPSILON))
    mask_float = channel_mask.astype(jnp.float32).T
    indices = (jnp.arange(L)[:, None] + jnp.arange(NOUT)[None, :]).astype(jnp.int32)

    def add_channel(stacked, inputs):
        series, scales, weights = inputs
        hankel = series.astype(jnp.float32)[indices]
        products = jnp.einsum('jt,kj->tk', hankel, tmpl_float, precision=lax.Precision.HIGHEST)
        return (stacked + products * scales[:, None] * weights[None, :], None)
    stacked, unused = lax.scan(add_channel, jnp.zeros((NOUT, K), jnp.float32), (aligned, data_scale, mask_float))
    return stacked * template_scale[None, :]
```

```python
import functools

import jax
import jax.numpy as jnp
from jax import lax
from jax.experimental import pallas as pl
from jax.experimental.pallas import tpu as pltpu
from jax.sharding import PartitionSpec as P

EPSILON = 1e-06
PH = 8
HALO = 128
VMEM = pl.BlockSpec(memory_space=pltpu.VMEM)
SMEM = pl.BlockSpec(memory_space=pltpu.SMEM)
BF = jnp.bfloat16
F32 = jnp.float32


def lane_iota(shape):
    return lax.broadcasted_iota(jnp.int32, shape, len(shape) - 1)


def row_iota(shape):
    return lax.broadcasted_iota(jnp.int32, shape, 0)


def whiten_kernel(raw_ref, halo_ref, taps_ref, out_ref):
    ext = jnp.concatenate([halo_ref[...], raw_ref[...]], axis=1)
    acc = raw_ref[...]
    for m in range(1, taps_ref.shape[1] + 1):
        acc = acc - taps_ref[:, m - 1 : m] * pltpu.roll(ext, m, 1)[:, HALO:]
    out_ref[...] = acc.astype(BF)


def shift_left(pieces, amount, lane):
    moved = [pltpu.roll(p, jnp.where(amount == 0, 0, 128 - amount), 1) for p in pieces]
    keep = lane < 128 - amount
    return [
        jnp.where(keep, moved[i], moved[(i + 1) % len(pieces)]) for i in range(len(pieces))
    ]


def shift_static(pieces, amount, lane):
    if amount == 0:
        return pieces
    moved = [pltpu.roll(p, 128 - amount, 1) for p in pieces]
    keep = lane < 128 - amount
    return [
        jnp.where(keep, moved[i], moved[(i + 1) % len(pieces)]) for i in range(len(pieces))
    ]


def band_setup(band_ref, b_ref):
    x = lane_iota((8, 128))
    s = row_iota((8, 128))
    residue = jnp.bitwise_and(8 - s, 7)
    band = jnp.broadcast_to(band_ref[...].astype(F32), (8, 128))
    left = jnp.where(jnp.bitwise_and(x, 7) == residue, band, 0.0).astype(BF)
    rx = row_iota((128, 128))
    rn = lane_iota((128, 128))
    right = (jnp.right_shift(rx + 16, 3) == rn).astype(F32).astype(BF)
    table = jnp.dot(left, right, preferred_element_type=F32)
    lane16 = lane_iota((16, 128))
    for v in range(PH):
        z = pltpu.roll(table, v, 0) if v else table
        z0 = pltpu.roll(z, 126, 1)
        z1 = pltpu.roll(z, 127, 1)
        upper = s <= v
        g = jnp.concatenate([jnp.where(upper, z0, z1), jnp.where(upper, z1, z)], axis=0)
        for pair in range(72):
            at = 2 * pair - 16
            turned = pltpu.roll(g, at % 128, 1) if at else g
            inside = (lane16 >= at) & (lane16 < at + 16)
            b_ref[16 * pair : 16 * pair + 16, 128 * v : 128 * v + 128] = jnp.where(
                inside, turned, 0.0
            ).astype(BF)


def stack_kernel(
    moveouts_ref, w_ref_in, band_ref, tmpl_ref, mask_ref, tail_ref, out_ref,
    b_ref, wide, f8, w_ref, h0, h1, q_ref, acc,
):
    channels = mask_ref.shape[1]
    count, length = tmpl_ref.shape
    rows = 512
    groups = rows // 128
    lane = lane_iota((8, 128))
    sub = row_iota((8, 128))

    tmpl = tmpl_ref[...]
    for t in range(PH):
        if t == 0:
            w_ref[0:count, :] = tmpl
        else:
            turned = pltpu.roll(tmpl.astype(F32), t, 1)
            w_ref[t * count : (t + 1) * count, :] = jnp.where(
                lane_iota((count, length)) >= t, turned, 0.0
            ).astype(BF)

    band_setup(band_ref, b_ref)
    tiles = w_ref_in.shape[1] // 1024
    for m in range(tiles):
        at = 64 * m
        if m == 0:
            wide[0:64, 0:HALO] = jnp.zeros((64, HALO), BF)
            wide[0:64, HALO:] = w_ref_in[:, 0:1024]
        else:
            wide[at : at + 64, :] = w_ref_in[:, 1024 * m - HALO : 1024 * m + 1024]
    for v in range(0, PH, 2):
        passed = jnp.dot(
            wide[...], b_ref[:, 128 * v : 128 * v + 256], preferred_element_type=F32
        ).astype(BF).astype(F32)
        for m in range(tiles):
            for e in range(2):
                f8[:, v + e, 128 * m : 128 * m + 128] = passed[
                    64 * m : 64 * m + 64, 128 * e : 128 * e + 128
                ]

    def prepare(c):
        move = moveouts_ref[c]
        move1 = jnp.right_shift(move, 3)
        move0 = jnp.bitwise_and(move, 7)
        whole = f8[c]
        x = [whole[:, 128 * i : 128 * i + 128] for i in range(5)]
        y = shift_left(x, move1, lane)
        y2 = shift_left(x, move1 + 1, lane)
        turn = jnp.bitwise_and(8 - move0, 7)
        near = sub < 8 - move0
        a = [jnp.where(near, pltpu.roll(p, turn, 0), pltpu.roll(q, turn, 0)) for p, q in zip(y, y2)]
        nxt = shift_static(a, 1, lane)
        a16 = jnp.concatenate(
            [jnp.concatenate([p, q], axis=0) for p, q in zip(a, nxt)], axis=1
        ).astype(BF)
        total = [p * p for p in a]
        for k in range(6):
            total = [p + q for p, q in zip(total, shift_static(total, 1 << k, lane))]
        after = shift_static(total, 1, lane)
        scales = []
        for i in range(groups):
            suffix = total[i]
            prefix = jnp.where(sub >= 1, pltpu.roll(after[i], 1, 0), 0.0)
            for k in (1, 2, 4):
                suffix = suffix + jnp.where(sub < 8 - k, pltpu.roll(suffix, 8 - k, 0), 0.0)
                prefix = prefix + jnp.where(sub >= k, pltpu.roll(prefix, k, 0), 0.0)
            scales.append(lax.rsqrt((suffix + prefix) / length + EPSILON))
        late = [pltpu.roll(p, 64, 1) for p in a]
        tail = [jnp.where(lane < 64, late[i], late[i + 1]) for i in range(groups)]
        return a16, scales, tail

    def build(a16, h_ref):
        for u in range(32):
            turned = pltpu.roll(a16, 640 - 2 * u, 1) if u else a16
            h_ref[16 * u : 16 * u + 16, :] = turned[:, :rows]

    def add_channel(h_ref, scales, c):
        mask = pltpu.roll(mask_ref[...], jnp.where(c == 0, 0, channels - c), 1)[:, 0:1]
        mask = jnp.broadcast_to(mask, (count, 128))
        for nt in range(2):
            r = jnp.dot(w_ref[...], h_ref[:, 256 * nt : 256 * nt + 256], preferred_element_type=F32)
            for t in range(PH):
                for g in range(2):
                    factor = mask * scales[2 * nt + g][t : t + 1, :]
                    at = (slice(count * t, count * t + count), slice(256 * nt + 128 * g, 256 * nt + 128 * g + 128))
                    acc[at] = acc[at] + r[count * t : count * t + count, 128 * g : 128 * g + 128] * factor

    acc[...] = jnp.zeros_like(acc)

    def pair(i, carry):
        c = 2 * i
        a16_0, s0, t0 = prepare(c)
        build(a16_0, h0)
        a16_1, s1, t1 = prepare(c + 1)
        build(a16_1, h1)
        add_channel(h0, s0, c)
        add_channel(h1, s1, c + 1)
        at = pl.multiple_of(16 * i, 16)
        for t in range(1, PH):
            q_ref[t - 1, pl.ds(at, 16), :] = jnp.concatenate(
                [
                    jnp.concatenate([t0[g] * s0[g][t : t + 1, :], t1[g] * s1[g][t : t + 1, :]], axis=0)
                    for g in range(groups)
                ],
                axis=1,
            ).astype(BF)
        return carry

    lax.fori_loop(0, channels // 2, pair, 0)

    wide_tmpl = tmpl.astype(F32)
    power = jnp.mean(wide_tmpl * wide_tmpl, axis=1, keepdims=True)
    gain = 1.0 / (length * jnp.sqrt(power + EPSILON))
    for t in range(PH):
        block = acc[count * t : count * t + count, :]
        if t:
            block = block + jnp.dot(tail_ref[t - 1], q_ref[t - 1], preferred_element_type=F32)
        block = block * gain
        out_ref[:, count * t : count * t + count] = block.T.astype(BF)


def shards(raw_data, whiten_taps, band_taps, templates, channel_mask, moveouts):
    channels, block_time = raw_data.shape
    count, length = templates.shape
    tm = lax.axis_size("tm")
    chan = lax.axis_size("chan")
    halo = lax.ppermute(
        raw_data[:, block_time - HALO :], "tm", [(q, q + 1) for q in range(tm - 1)]
    )
    white = pl.pallas_call(
        whiten_kernel,
        out_shape=jax.ShapeDtypeStruct((channels, block_time), BF),
        in_specs=[VMEM] * 3,
        out_specs=VMEM,
    )(raw_data, halo, whiten_taps)
    white = lax.all_gather(white, "tm", axis=1, tiled=True)

    mask = channel_mask.astype(BF)
    spread = jnp.repeat(mask, PH, axis=1)
    tails = []
    for t in range(1, PH):
        last = jnp.pad(templates[:, length - t :], ((0, 0), (0, PH - t)))
        tails.append(jnp.tile(last, (1, channels)) * spread)
    tails = jnp.stack(tails)
    band = jnp.pad(band_taps, (0, 128 - band_taps.shape[0])).reshape(1, 128)

    partial = pl.pallas_call(
        stack_kernel,
        out_shape=jax.ShapeDtypeStruct((512, PH * count), BF),
        in_specs=[SMEM] + [VMEM] * 5,
        out_specs=VMEM,
        scratch_shapes=[
            pltpu.VMEM((1152, 1024), BF),
            pltpu.VMEM((320, 1152), BF),
            pltpu.VMEM((64, 8, 640), F32),
            pltpu.VMEM((512, 512), BF),
            pltpu.VMEM((512, 512), BF),
            pltpu.VMEM((512, 512), BF),
            pltpu.VMEM((7, 512, 512), BF),
            pltpu.VMEM((512, 512), F32),
        ],
        compiler_params=pltpu.CompilerParams(vmem_limit_bytes=40 * 2**20),
    )(moveouts, white, band, templates, channel_mask.astype(F32), tails)
    parts = lax.all_to_all(partial, "chan", 0, 0, tiled=True)
    total = jnp.sum(parts.reshape(chan, 512 // chan, PH * count).astype(F32), axis=0)
    return total.reshape(512 // chan * PH, count)


def solution(mesh):
    in_specs = (P("chan", "tm"), P("chan", None), P(), P("tm", None), P("tm", "chan"), P("chan"))
    out_specs = P("chan", "tm")
    return jax.shard_map(shards, mesh=mesh, in_specs=in_specs, out_specs=out_specs, check_vma=False)
```

```python
import functools

import jax
import jax.numpy as jnp
from jax import lax
from jax.experimental import pallas as pl
from jax.experimental.pallas import tpu as pltpu
from jax.sharding import PartitionSpec as P

EPSILON = 1e-06
GROUP = 8
UNROLL = 4
FIRST = (1, 4, 5)
SECOND = (2, 8, 10)
PH = 8
HALO = 128
VMEM = pl.BlockSpec(memory_space=pltpu.VMEM)
SMEM = pl.BlockSpec(memory_space=pltpu.SMEM)
BF = jnp.bfloat16
F32 = jnp.float32


def lane_iota(shape):
    return lax.broadcasted_iota(jnp.int32, shape, len(shape) - 1)


def row_iota(shape):
    return lax.broadcasted_iota(jnp.int32, shape, 0)


def whiten_kernel(raw_ref, halo_ref, taps_ref, out_ref):
    taps = taps_ref[...].T
    for at in range(0, raw_ref.shape[0], 16):
        halves = []
        for row in (at, at + 8):
            rows = slice(row, row + 8)
            ext = jnp.concatenate([halo_ref[rows, :], raw_ref[rows, :]], axis=1)
            acc = raw_ref[rows, :]
            for m in range(1, taps.shape[1] + 1):
                acc = acc - taps[rows, m - 1 : m] * pltpu.roll(ext, m, 1)[:, HALO:]
            halves.append(acc)
        out_ref[at : at + 16, :] = jnp.concatenate(halves, axis=0).astype(BF)


def shift_left(pieces, amount, lane):
    moved = [pltpu.roll(p, jnp.where(amount == 0, 0, 128 - amount), 1) for p in pieces]
    keep = lane < 128 - amount
    return [
        jnp.where(keep, moved[i], moved[(i + 1) % len(pieces)]) for i in range(len(pieces))
    ]


def shift_static(pieces, amount, lane):
    if amount == 0:
        return pieces
    moved = [pltpu.roll(p, 128 - amount, 1) for p in pieces]
    keep = lane < 128 - amount
    return [
        jnp.where(keep, moved[i], moved[(i + 1) % len(pieces)]) for i in range(len(pieces))
    ]


def band_setup(band_ref, b_ref):
    x = lane_iota((8, 128))
    s = row_iota((8, 128))
    residue = jnp.bitwise_and(8 - s, 7)
    band = jnp.broadcast_to(band_ref[...].astype(F32), (8, 128))
    left = jnp.where(jnp.bitwise_and(x, 7) == residue, band, 0.0).astype(BF)
    rx = row_iota((128, 128))
    rn = lane_iota((128, 128))
    right = (jnp.right_shift(rx + 16, 3) == rn).astype(F32).astype(BF)
    table = jnp.dot(left, right, preferred_element_type=F32)
    lane16 = lane_iota((16, 128))
    for v in range(PH):
        z = pltpu.roll(table, v, 0) if v else table
        z0 = pltpu.roll(z, 126, 1)
        z1 = pltpu.roll(z, 127, 1)
        upper = s <= v
        g = jnp.concatenate([jnp.where(upper, z0, z1), jnp.where(upper, z1, z)], axis=0)
        for pair in range(72):
            at = 2 * pair - 16
            turned = pltpu.roll(g, at % 128, 1) if at else g
            inside = (lane16 >= at) & (lane16 < at + 16)
            b_ref[16 * pair : 16 * pair + 16, 128 * v : 128 * v + 128] = jnp.where(
                inside, turned, 0.0
            ).astype(BF)


def setup_kernel(band_ref, tmpl_ref, b_ref, w_ref):
    count, length = tmpl_ref.shape
    wide_tmpl = tmpl_ref[...].astype(F32)
    w_ref[0:count, :] = tmpl_ref[...]
    for t in range(1, PH):
        w_ref[t * count : (t + 1) * count, :] = jnp.where(
            lane_iota((count, length)) >= t, pltpu.roll(wide_tmpl, t, 1), 0.0
        ).astype(BF)
    band_setup(band_ref, b_ref)


def spread_masks(tmpl_ref, mask_ref, ones_ref, tail_ref, m_ref):
    count, length = tmpl_ref.shape
    channels = mask_ref.shape[1]
    ri = row_iota((640, 640))
    ci = lane_iota((640, 640))
    ones_ref[...] = ((ri >= ci) & (ri < ci + 64)).astype(F32).astype(BF)
    mask = mask_ref[...].astype(F32).astype(BF)
    wide = 128 * 8
    for block in range(channels // 8):
        pick = row_iota((channels, wide)) == 8 * block + jnp.right_shift(lane_iota((channels, wide)), 7)
        spread = jnp.dot(mask, pick.astype(F32).astype(BF), preferred_element_type=F32).astype(BF)
        for k in range(8):
            m_ref[8 * block + k] = spread[:, 128 * k : 128 * k + 128]
    lanes = channels * PH
    repeat = row_iota((channels, lanes)) == jnp.right_shift(lane_iota((channels, lanes)), 3)
    spread = jnp.dot(mask, repeat.astype(F32).astype(BF), preferred_element_type=F32)
    v = jnp.bitwise_and(lane_iota((128, lanes)), PH - 1)
    j = row_iota((128, lanes))
    for t in range(1, PH):
        pick = (j == 128 - t + v) & (v < t)
        last = jnp.dot(
            tmpl_ref[:, length - 128 :], pick.astype(F32).astype(BF), preferred_element_type=F32
        )
        tail_ref[t - 1] = (last * spread).astype(BF)


def stack_kernel(place_ref, moveouts_ref, *refs):
    blocks = refs[:8]
    (tmpl_ref, mask_ref, b_ref, w_ref, keep_ref, *send_refs) = refs[8:16]
    (white, wide, f8, ones_ref, tail_ref, m_ref, h0, h1, a_ref, s_ref, q_ref, acc,
     high_ref, low_ref, tail_rows, sums, turned) = refs[16:]
    channels, _, rows = s_ref.shape
    count, length = tmpl_ref.shape
    groups = rows // 128
    lane = lane_iota((8, 128))
    sub = row_iota((8, 128))
    spread_masks(tmpl_ref, mask_ref, ones_ref, tail_ref, m_ref)

    me = place_ref[0]
    block_time = blocks[0].shape[1]
    white[:, 0:HALO] = jnp.zeros((64, HALO), BF)
    for k in range(8):
        chip = jnp.bitwise_and(jnp.right_shift(me, 1) + (k & 3), 3)
        core = jnp.bitwise_xor(jnp.bitwise_and(me, 1), k >> 2)
        at = pl.multiple_of(HALO + block_time * (2 * chip + core), 128)
        white[:, pl.ds(at, block_time)] = blocks[k][...]

    tiles = 5
    for m in range(tiles):
        wide[64 * m : 64 * m + 64, :] = white[:, 1024 * m : 1024 * m + 1024 + HALO]
    for v in range(0, PH, 2):
        passed = jnp.dot(
            wide[...], b_ref[:, 128 * v : 128 * v + 256], preferred_element_type=F32
        ).astype(BF).astype(F32)
        for m in range(tiles):
            for e in range(2):
                f8[:, v + e, 128 * m : 128 * m + 128] = passed[
                    64 * m : 64 * m + 64, 128 * e : 128 * e + 128
                ]

    def align(c):
        move = moveouts_ref[c]
        move1 = jnp.right_shift(move, 3)
        move0 = jnp.bitwise_and(move, 7)
        turn = jnp.bitwise_and(8 - move0, 7)
        near = sub < 8 - move0
        whole = f8[c]
        x = [pltpu.roll(whole[:, 128 * i : 128 * i + 128], turn, 0) for i in range(5)]
        y0 = shift_left(x, move1, lane)
        y1 = shift_static(y0, 1, lane)
        y2 = shift_static(y1, 1, lane)
        a = [jnp.where(near, p, q) for p, q in zip(y0, y1)]
        nxt = [jnp.where(near, p, q) for p, q in zip(y1, y2)]
        a_ref[c] = jnp.concatenate(
            [jnp.concatenate([p, q], axis=0) for p, q in zip(a, nxt)], axis=1
        ).astype(BF)
        return jnp.concatenate(a, axis=1)

    def first(i, carry):
        for e in range(0, GROUP, 2):
            c = GROUP * i + e
            both = jnp.concatenate([align(c), align(c + 1)], axis=0)
            square = both * both
            high = square.astype(BF)
            at = pl.ds(pl.multiple_of(8 * c, 16), 16)
            high_ref[at, :] = high
            low_ref[at, :] = (square - high.astype(F32)).astype(BF)
            tail_rows[at, :] = pltpu.roll(both.astype(BF), 640 - 64, 1)[:, :rows]
        return carry

    lax.fori_loop(0, channels // GROUP, first, 0)

    for half in range(2):
        at = slice(256 * half, 256 * half + 256)
        sums[at, :] = jnp.dot(
            high_ref[at, :], ones_ref[...], preferred_element_type=F32
        ) + jnp.dot(low_ref[at, :], ones_ref[...], preferred_element_type=F32)

    def second(i, carry):
        for e in range(0, GROUP, 2):
            pair_scales = []
            for k in range(2):
                c = GROUP * i + e + k
                whole = sums[pl.ds(pl.multiple_of(8 * c, 8), 8), :]
                total = [whole[:, 128 * g : 128 * g + 128] for g in range(5)]
                after = shift_static(total, 1, lane)
                scales = []
                for g in range(groups):
                    suffix = total[g]
                    prefix = jnp.where(sub >= 1, pltpu.roll(after[g], 1, 0), 0.0)
                    for step in (1, 2, 4):
                        suffix = suffix + jnp.where(sub < 8 - step, pltpu.roll(suffix, 8 - step, 0), 0.0)
                        prefix = prefix + jnp.where(sub >= step, pltpu.roll(prefix, step, 0), 0.0)
                    scales.append(lax.rsqrt((suffix + prefix) / length + EPSILON))
                scales = jnp.concatenate(scales, axis=1)
                s_ref[c] = scales
                pair_scales.append(scales)
            at = pl.ds(pl.multiple_of(8 * (GROUP * i + e), 16), 16)
            tail = tail_rows[at, :].astype(F32)
            for t in range(1, PH):
                q_ref[t - 1, at, :] = jnp.concatenate(
                    [tail[8 * k : 8 * k + 8] * pair_scales[k][t : t + 1, :] for k in range(2)], axis=0
                ).astype(BF)
        return carry

    lax.fori_loop(0, channels // GROUP, second, 0)
    keep = lane_iota((16, 128))

    def build(c, h_ref):
        x = a_ref[c]
        for u in range(32):
            for g in range(groups):
                p, q = x[:, 128 * g : 128 * g + 128], x[:, 128 * g + 128 : 128 * g + 256]
                if u:
                    p = pltpu.roll(jnp.where(keep >= 2 * u, p, q), 128 - 2 * u, 1)
                h_ref[16 * u : 16 * u + 16, 128 * g : 128 * g + 128] = p

    def add_channel(h_ref, c):
        mask = m_ref[c].astype(F32)
        for nt in range(2):
            lanes = slice(256 * nt, 256 * nt + 256)
            for half in range(2):
                r = jnp.dot(
                    w_ref[256 * half : 256 * half + 256, :], h_ref[:, lanes], preferred_element_type=F32
                )
                for t in range(4):
                    for g in range(2):
                        col = slice(256 * nt + 128 * g, 256 * nt + 128 * g + 128)
                        row = 4 * half + t
                        at = (slice(count * row, count * row + count), col)
                        part = r[count * t : count * t + count, 128 * g : 128 * g + 128]
                        acc[at] = acc[at] + part * (mask * s_ref[c, row : row + 1, col])

    acc[...] = jnp.zeros_like(acc)
    build(0, h0)

    def several(i, carry):
        for k in range(0, UNROLL, 2):
            c = UNROLL * i + k
            build(c + 1, h1)
            add_channel(h0, c)
            build(jnp.minimum(c + 2, channels - 1), h0)
            add_channel(h1, c + 1)
        return carry

    lax.fori_loop(0, channels // UNROLL, several, 0)

    wide_tmpl = tmpl_ref[...].astype(F32)
    power = jnp.mean(wide_tmpl * wide_tmpl, axis=1, keepdims=True)
    gain = 1.0 / (length * jnp.sqrt(power + EPSILON))
    for t in range(PH):
        at = slice(count * t, count * t + count)
        block = acc[at, :]
        if t:
            block = block + jnp.dot(tail_ref[t - 1], q_ref[t - 1], preferred_element_type=F32)
        turned[:, at] = (block * gain).T
    home = place_ref[1]
    for first_flip, ref in zip((0,) + FIRST, (keep_ref, *send_refs)):
        for p, second_flip in enumerate((0,) + SECOND):
            owner = jnp.bitwise_xor(home, first_flip ^ second_flip)
            part = turned[pl.ds(pl.multiple_of(32 * owner, 32), 32), :]
            ref[32 * p : 32 * p + 32, :] = part.astype(ref.dtype)


def gather_time(white):
    own = [white]
    for d in (1, 2, 3):
        own.append(lax.ppermute(white, "tm", [((q + 2 * d) % 8, q) for q in range(8)]))
    other = [lax.ppermute(p, "tm", [(q ^ 1, q) for q in range(8)]) for p in own]
    return own + other


def swap(value, flip):
    return lax.ppermute(value, "chan", [(i, i ^ flip) for i in range(lax.axis_size("chan"))])


def reduce_lags(kept, sent):
    total = kept
    for part, flip in zip([swap(p, f) for p, f in zip(sent, FIRST)], FIRST):
        total = total + part.astype(F32)
    narrow = total.astype(BF)
    rows = total.shape[0] // 4
    total = total[:rows]
    for k, flip in enumerate(SECOND):
        total = total + swap(narrow[rows * k + rows : rows * k + 2 * rows], flip).astype(F32)
    return total


def shards(raw_data, whiten_taps, band_taps, templates, channel_mask, moveouts):
    channels, block_time = raw_data.shape
    count, length = templates.shape
    tm = lax.axis_size("tm")
    halo = lax.ppermute(
        raw_data[:, block_time - HALO :], "tm", [(q, q + 1) for q in range(tm - 1)]
    )
    band = jnp.pad(band_taps, (0, 128 - band_taps.shape[0])).reshape(1, 128)
    b, w = pl.pallas_call(
        setup_kernel,
        out_shape=[
            jax.ShapeDtypeStruct((1152, 1024), BF),
            jax.ShapeDtypeStruct((512, 512), BF),
        ],
        in_specs=[VMEM] * 2,
        out_specs=[VMEM] * 2,
        cost_estimate=pl.CostEstimate(flops=2**31, bytes_accessed=2**22, transcendentals=0),
        compiler_params=pltpu.CompilerParams(vmem_limit_bytes=8 * 2**20),
    )(band, templates)
    white = pl.pallas_call(
        whiten_kernel,
        out_shape=jax.ShapeDtypeStruct((channels, block_time), BF),
        in_specs=[VMEM] * 3,
        out_specs=VMEM,
    )(raw_data, halo, whiten_taps.T)
    blocks = gather_time(white)
    place = jnp.stack([lax.axis_index("tm"), lax.axis_index("chan")]).astype(jnp.int32)
    kept, *sent = pl.pallas_call(
        stack_kernel,
        out_shape=[jax.ShapeDtypeStruct((128, PH * count), F32)]
        + [jax.ShapeDtypeStruct((128, PH * count), BF)] * 3,
        in_specs=[SMEM] * 2 + [VMEM] * 12,
        out_specs=[VMEM] * 4,
        scratch_shapes=[
            pltpu.VMEM((64, HALO + 5120), BF),
            pltpu.VMEM((320, 1152), BF),
            pltpu.VMEM((64, 8, 640), F32),
            pltpu.VMEM((640, 640), BF),
            pltpu.VMEM((7, 64, 512), BF),
            pltpu.VMEM((64, 64, 128), BF),
            pltpu.VMEM((512, 512), BF),
            pltpu.VMEM((512, 512), BF),
            pltpu.VMEM((64, 16, 640), BF),
            pltpu.VMEM((64, 8, 512), F32),
            pltpu.VMEM((7, 512, 512), BF),
            pltpu.VMEM((512, 512), F32),
            pltpu.VMEM((512, 640), BF),
            pltpu.VMEM((512, 640), BF),
            pltpu.VMEM((512, 512), BF),
            pltpu.VMEM((512, 640), F32),
            pltpu.VMEM((512, 512), F32),
        ],
        cost_estimate=pl.CostEstimate(flops=2**34, bytes_accessed=2**23, transcendentals=0),
        compiler_params=pltpu.CompilerParams(vmem_limit_bytes=30 * 2**20),
    )(place, moveouts, *blocks, templates, channel_mask, b, w)
    return reduce_lags(kept, sent).reshape(256, count)


def solution(mesh):
    in_specs = (P("chan", "tm"), P("chan", None), P(), P("tm", None), P("tm", "chan"), P("chan"))
    out_specs = P("chan", "tm")
    return jax.shard_map(shards, mesh=mesh, in_specs=in_specs, out_specs=out_specs, check_vma=False)
```

```python
import functools

import jax
import jax.numpy as jnp
from jax import lax
from jax.experimental import pallas as pl
from jax.experimental.pallas import tpu as pltpu
from jax.sharding import PartitionSpec as P

EPSILON = 1e-06
GROUP = 8
UNROLL = 4
FIRST = (1, 3, 2)
SECOND = (4, 12, 8)
PH = 8
HALO = 128
VMEM = pl.BlockSpec(memory_space=pltpu.VMEM)
SMEM = pl.BlockSpec(memory_space=pltpu.SMEM)
BF = jnp.bfloat16
F32 = jnp.float32


def lane_iota(shape):
    return lax.broadcasted_iota(jnp.int32, shape, len(shape) - 1)


def row_iota(shape):
    return lax.broadcasted_iota(jnp.int32, shape, 0)


def whiten_kernel(raw_ref, taps_ref, out_ref):
    taps = taps_ref[...].T
    lane = lane_iota((8, 128))
    width = raw_ref.shape[1]
    for at in range(0, raw_ref.shape[0], 16):
        halves = []
        for row in (at, at + 8):
            rows = slice(row, row + 8)
            raw = [raw_ref[rows, k : k + 128] for k in range(0, width, 128)]
            pieces = [jnp.zeros((8, 128), F32)] + raw
            acc = raw
            for m in range(1, taps.shape[1] + 1):
                tap = taps[rows, m - 1 : m]
                acc = [
                    acc[i] - tap * pltpu.roll(jnp.where(lane < 128 - m, pieces[i + 1], pieces[i]), m, 1)
                    for i in range(len(raw))
                ]
            edge = jnp.where(lane < 16, pltpu.roll(raw[-1], 16, 1), pltpu.roll(acc[0], 16, 1))
            edge = jnp.where(lane < 32, edge, 0.0)
            high = edge.astype(BF).astype(F32)
            middle = (edge - high).astype(BF).astype(F32)
            low = edge - high - middle
            edge = high + pltpu.roll(middle, 32, 1) + pltpu.roll(low, 64, 1)
            halves.append(jnp.concatenate(acc + [edge], axis=1))
        out_ref[at : at + 16, :] = jnp.concatenate(halves, axis=0).astype(BF)


def shift_left(pieces, amount, lane):
    moved = [pltpu.roll(p, jnp.where(amount == 0, 0, 128 - amount), 1) for p in pieces]
    keep = lane < 128 - amount
    return [
        jnp.where(keep, moved[i], moved[(i + 1) % len(pieces)]) for i in range(len(pieces))
    ]


def shift_static(pieces, amount, lane):
    if amount == 0:
        return pieces
    moved = [pltpu.roll(p, 128 - amount, 1) for p in pieces]
    keep = lane < 128 - amount
    return [
        jnp.where(keep, moved[i], moved[(i + 1) % len(pieces)]) for i in range(len(pieces))
    ]


def band_setup(band_ref, b_ref):
    x = lane_iota((8, 128))
    s = row_iota((8, 128))
    residue = jnp.bitwise_and(8 - s, 7)
    taps = band_ref[...].astype(F32)
    taps = jnp.concatenate([taps, jnp.zeros((1, 128 - taps.shape[1]), F32)], axis=1)
    band = jnp.broadcast_to(taps, (8, 128))
    left = jnp.where(jnp.bitwise_and(x, 7) == residue, band, 0.0).astype(BF)
    rx = row_iota((128, 128))
    rn = lane_iota((128, 128))
    right = (jnp.right_shift(rx + 16, 3) == rn).astype(F32).astype(BF)
    table = jnp.dot(left, right, preferred_element_type=F32)
    lane16 = lane_iota((16, 128))
    for v in range(PH):
        z = pltpu.roll(table, v, 0) if v else table
        z0 = pltpu.roll(z, 126, 1)
        z1 = pltpu.roll(z, 127, 1)
        upper = s <= v
        g = jnp.concatenate([jnp.where(upper, z0, z1), jnp.where(upper, z1, z)], axis=0)
        for pair in range(72):
            at = 2 * pair - 16
            turned = pltpu.roll(g, at % 128, 1) if at else g
            inside = (lane16 >= at) & (lane16 < at + 16)
            b_ref[16 * pair : 16 * pair + 16, 128 * v : 128 * v + 128] = jnp.where(
                inside, turned, 0.0
            ).astype(BF)


def setup_kernel(band_ref, tmpl_ref, b_ref, w_ref):
    count, length = tmpl_ref.shape
    wide_tmpl = tmpl_ref[...].astype(F32)
    w_ref[0:count, :] = tmpl_ref[...]
    for t in range(1, PH):
        w_ref[t * count : (t + 1) * count, :] = jnp.where(
            lane_iota((count, length)) >= t, pltpu.roll(wide_tmpl, t, 1), 0.0
        ).astype(BF)
    band_setup(band_ref, b_ref)


def spread_masks(tmpl_ref, mask_ref, ones_ref, tail_ref, m_ref):
    count, length = tmpl_ref.shape
    channels = mask_ref.shape[1]
    ri = row_iota((384, 256))
    ci = lane_iota((384, 256))
    ones_ref[...] = ((ri >= ci) & (ri < ci + 64)).astype(F32).astype(BF)
    mask = mask_ref[...].astype(F32).astype(BF)
    wide = 128 * 8
    for block in range(channels // 8):
        pick = row_iota((channels, wide)) == 8 * block + jnp.right_shift(lane_iota((channels, wide)), 7)
        spread = jnp.dot(mask, pick.astype(F32).astype(BF), preferred_element_type=F32).astype(BF)
        for k in range(8):
            m_ref[8 * block + k] = spread[:, 128 * k : 128 * k + 128]
    lanes = channels * PH
    repeat = row_iota((channels, lanes)) == jnp.right_shift(lane_iota((channels, lanes)), 3)
    spread = jnp.dot(mask, repeat.astype(F32).astype(BF), preferred_element_type=F32)
    v = jnp.bitwise_and(lane_iota((128, lanes)), PH - 1)
    j = row_iota((128, lanes))
    for t in range(1, PH):
        pick = (j == 128 - t + v) & (v < t)
        last = jnp.dot(
            tmpl_ref[:, length - 128 :], pick.astype(F32).astype(BF), preferred_element_type=F32
        )
        tail_ref[t - 1] = (last * spread).astype(BF)


def stack_kernel(place_ref, moveouts_ref, *refs):
    blocks = refs[:8]
    (tmpl_ref, mask_ref, taps_ref, b_ref, w_ref, keep_ref, *send_refs) = refs[8:17]
    (white, edges, wide, f8, ones_ref, tail_ref, m_ref, h0, h1, a_ref, s_ref, q_ref, acc,
     high_ref, low_ref, tail_rows, sums, turned) = refs[17:]
    channels, _, rows = s_ref.shape
    count, length = tmpl_ref.shape
    groups = rows // 128
    lane = lane_iota((8, 128))
    sub = row_iota((8, 128))
    spread_masks(tmpl_ref, mask_ref, ones_ref, tail_ref, m_ref)

    me = place_ref[0]
    block_time = blocks[0].shape[1] - 128
    white[:, 0:HALO] = jnp.zeros((64, HALO), BF)
    for k in range(8):
        chip = jnp.bitwise_and(jnp.right_shift(me, 1) + (k & 3), 3)
        core = jnp.bitwise_xor(jnp.bitwise_and(me, 1), k >> 2)
        when = 2 * chip + core
        at = pl.multiple_of(HALO + block_time * when, 128)
        white[:, pl.ds(at, block_time)] = blocks[k][:, 0:block_time]
        edge = blocks[k][:, block_time:].astype(F32)
        edges[when] = edge + pltpu.roll(edge, 96, 1) + pltpu.roll(edge, 64, 1)

    taps = taps_ref[...].T
    for at in range(0, 64, 16):
        fixed = []
        for row in (at, at + 8):
            rows16 = slice(row, row + 8)
            both = []
            for quad in range(2):
                start = jnp.zeros((8, 128), F32)
                before = jnp.zeros((8, 128), F32)
                for k in range(4):
                    when = 4 * quad + k
                    own = edges[when, rows16, :]
                    start = jnp.where((lane >= 32 * k + 16) & (lane < 32 * k + 32), pltpu.roll(own, 32 * k, 1) if k else own, start)
                    if when:
                        last = edges[when - 1, rows16, :]
                        before = jnp.where((lane >= 32 * k) & (lane < 32 * k + 16), pltpu.roll(last, 32 * k, 1) if k else last, before)
                for m in range(1, taps.shape[1] + 1):
                    start = start - taps[rows16, m - 1 : m] * pltpu.roll(before, m, 1)
                both.append(start)
            fixed.append(both)
        for when in range(1, 8):
            quad, k = when >> 2, when & 3
            first16 = jnp.concatenate([fixed[0][quad], fixed[1][quad]], axis=0)
            first16 = pltpu.roll(first16, (112 - 32 * k) % 128, 1)
            cols = slice(HALO + block_time * when, HALO + block_time * when + 128)
            old = white[at : at + 16, cols].astype(F32)
            white[at : at + 16, cols] = jnp.where(lane_iota((16, 128)) < 16, first16, old).astype(BF)

    tiles = 5
    for m in range(tiles):
        wide[64 * m : 64 * m + 64, :] = white[:, 1024 * m : 1024 * m + 1024 + HALO]
    for v in range(0, PH, 2):
        passed = jnp.dot(
            wide[...], b_ref[:, 128 * v : 128 * v + 256], preferred_element_type=F32
        ).astype(BF).astype(F32)
        for m in range(tiles):
            for e in range(2):
                f8[:, v + e, 128 * m : 128 * m + 128] = passed[
                    64 * m : 64 * m + 64, 128 * e : 128 * e + 128
                ]

    def align(c):
        move = moveouts_ref[c]
        move1 = jnp.right_shift(move, 3)
        move0 = jnp.bitwise_and(move, 7)
        turn = jnp.bitwise_and(8 - move0, 7)
        near = sub < 8 - move0
        whole = f8[c]
        x = [pltpu.roll(whole[:, 128 * i : 128 * i + 128], turn, 0) for i in range(5)]
        y0 = shift_left(x, move1, lane)
        y1 = shift_static(y0, 1, lane)
        y2 = shift_static(y1, 1, lane)
        a = [jnp.where(near, p, q) for p, q in zip(y0, y1)]
        nxt = [jnp.where(near, p, q) for p, q in zip(y1, y2)]
        a_ref[c] = jnp.concatenate(
            [jnp.concatenate([p, q], axis=0) for p, q in zip(a, nxt)], axis=1
        ).astype(BF)
        return jnp.concatenate(a, axis=1)

    def first(i, carry):
        for e in range(0, GROUP, 2):
            c = GROUP * i + e
            both = jnp.concatenate([align(c), align(c + 1)], axis=0)
            square = both * both
            high = square.astype(BF)
            at = pl.ds(pl.multiple_of(8 * c, 16), 16)
            high_ref[at, :] = high
            low_ref[at, :] = (square - high.astype(F32)).astype(BF)
            tail_rows[at, :] = pltpu.roll(both.astype(BF), 640 - 64, 1)[:, :rows]
        return carry

    lax.fori_loop(0, channels // GROUP, first, 0)

    for half in range(2):
        at = slice(256 * half, 256 * half + 384)
        sums[:, 256 * half : 256 * half + 256] = jnp.dot(
            high_ref[:, at], ones_ref[...], preferred_element_type=F32
        ) + jnp.dot(low_ref[:, at], ones_ref[...], preferred_element_type=F32)
    last = high_ref[:, 512:640].astype(F32) + low_ref[:, 512:640].astype(F32)
    last = jnp.sum(jnp.where(lane_iota((512, 128)) < 64, last, 0.0), axis=1, keepdims=True)
    sums[:, 512:640] = jnp.broadcast_to(last, (512, 128))

    def second(i, carry):
        for e in range(0, GROUP, 2):
            pair_scales = []
            for k in range(2):
                c = GROUP * i + e + k
                whole = sums[pl.ds(pl.multiple_of(8 * c, 8), 8), :]
                total = [whole[:, 128 * g : 128 * g + 128] for g in range(5)]
                after = shift_static(total, 1, lane)
                scales = []
                for g in range(groups):
                    suffix = total[g]
                    prefix = jnp.where(sub >= 1, pltpu.roll(after[g], 1, 0), 0.0)
                    for step in (1, 2, 4):
                        suffix = suffix + jnp.where(sub < 8 - step, pltpu.roll(suffix, 8 - step, 0), 0.0)
                        prefix = prefix + jnp.where(sub >= step, pltpu.roll(prefix, step, 0), 0.0)
                    scales.append(lax.rsqrt((suffix + prefix) / length + EPSILON))
                scales = jnp.concatenate(scales, axis=1)
                s_ref[c] = scales
                pair_scales.append(scales)
            at = pl.ds(pl.multiple_of(8 * (GROUP * i + e), 16), 16)
            tail = tail_rows[at, :].astype(F32)
            for t in range(1, PH):
                q_ref[t - 1, at, :] = jnp.concatenate(
                    [tail[8 * k : 8 * k + 8] * pair_scales[k][t : t + 1, :] for k in range(2)], axis=0
                ).astype(BF)
        return carry

    lax.fori_loop(0, channels // GROUP, second, 0)
    keep = lane_iota((16, 128))

    def build(c, h_ref):
        x = a_ref[c]
        for u in range(32):
            for g in range(groups):
                p, q = x[:, 128 * g : 128 * g + 128], x[:, 128 * g + 128 : 128 * g + 256]
                if u:
                    p = pltpu.roll(jnp.where(keep >= 2 * u, p, q), 128 - 2 * u, 1)
                h_ref[16 * u : 16 * u + 16, 128 * g : 128 * g + 128] = p

    def add_channel(h_ref, c):
        mask = m_ref[c].astype(F32)
        for nt in range(2):
            lanes = slice(256 * nt, 256 * nt + 256)
            for half in range(2):
                r = jnp.dot(
                    w_ref[256 * half : 256 * half + 256, :], h_ref[:, lanes], preferred_element_type=F32
                )
                for t in range(4):
                    for g in range(2):
                        col = slice(256 * nt + 128 * g, 256 * nt + 128 * g + 128)
                        row = 4 * half + t
                        at = (slice(count * row, count * row + count), col)
                        part = r[count * t : count * t + count, 128 * g : 128 * g + 128]
                        acc[at] = acc[at] + part * (mask * s_ref[c, row : row + 1, col])

    acc[...] = jnp.zeros_like(acc)
    build(0, h0)

    def several(i, carry):
        for k in range(0, UNROLL, 2):
            c = UNROLL * i + k
            build(c + 1, h1)
            add_channel(h0, c)
            build(jnp.minimum(c + 2, channels - 1), h0)
            add_channel(h1, c + 1)
        return carry

    lax.fori_loop(0, channels // UNROLL, several, 0)

    wide_tmpl = tmpl_ref[...].astype(F32)
    power = jnp.mean(wide_tmpl * wide_tmpl, axis=1, keepdims=True)
    gain = 1.0 / (length * jnp.sqrt(power + EPSILON))
    for t in range(PH):
        at = slice(count * t, count * t + count)
        block = acc[at, :]
        if t:
            block = block + jnp.dot(tail_ref[t - 1], q_ref[t - 1], preferred_element_type=F32)
        turned[:, at] = (block * gain).T
    home = place_ref[1]
    for first_flip, ref in zip((0,) + FIRST, (keep_ref, *send_refs)):
        for p, second_flip in enumerate((0,) + SECOND):
            owner = jnp.bitwise_xor(home, first_flip ^ second_flip)
            part = turned[pl.ds(pl.multiple_of(32 * owner, 32), 32), :]
            ref[32 * p : 32 * p + 32, :] = part.astype(ref.dtype)


def gather_time(white):
    own = [white]
    for d in (1, 2, 3):
        own.append(lax.ppermute(white, "tm", [((q + 2 * d) % 8, q) for q in range(8)]))
    other = [lax.ppermute(p, "tm", [(q ^ 1, q) for q in range(8)]) for p in own]
    return own + other


def swap(value, flip):
    return lax.ppermute(value, "chan", [(i, i ^ flip) for i in range(lax.axis_size("chan"))])


def reduce_lags(kept, sent):
    total = kept
    for part, flip in zip([swap(p, f) for p, f in zip(sent, FIRST)], FIRST):
        total = total + part.astype(F32)
    narrow = total.astype(BF)
    rows = total.shape[0] // 4
    total = total[:rows]
    for k, flip in enumerate(SECOND):
        total = total + swap(narrow[rows * k + rows : rows * k + 2 * rows], flip).astype(F32)
    return total


def shards(raw_data, whiten_taps, band_taps, templates, channel_mask, moveouts):
    channels, block_time = raw_data.shape
    count, length = templates.shape
    white = pl.pallas_call(
        whiten_kernel,
        out_shape=jax.ShapeDtypeStruct((channels, block_time + 128), BF),
        in_specs=[VMEM] * 2,
        out_specs=VMEM,
        compiler_params=pltpu.CompilerParams(vmem_limit_bytes=4 * 2**20),
    )(raw_data, whiten_taps.T)
    b, w = pl.pallas_call(
        setup_kernel,
        out_shape=[
            jax.ShapeDtypeStruct((1152, 1024), BF),
            jax.ShapeDtypeStruct((512, 512), BF),
        ],
        in_specs=[VMEM] * 2,
        out_specs=[VMEM] * 2,
        cost_estimate=pl.CostEstimate(flops=2**31, bytes_accessed=2**22, transcendentals=0),
        compiler_params=pltpu.CompilerParams(vmem_limit_bytes=8 * 2**20),
    )(band_taps.reshape(1, -1), templates)
    blocks = gather_time(white)
    place = jnp.stack([lax.axis_index("tm"), lax.axis_index("chan")]).astype(jnp.int32)
    kept, *sent = pl.pallas_call(
        stack_kernel,
        out_shape=[jax.ShapeDtypeStruct((128, PH * count), F32)]
        + [jax.ShapeDtypeStruct((128, PH * count), BF)] * 3,
        in_specs=[SMEM] * 2 + [VMEM] * 13,
        out_specs=[VMEM] * 4,
        scratch_shapes=[
            pltpu.VMEM((64, HALO + 5120), BF),
            pltpu.VMEM((8, 64, 128), F32),
            pltpu.VMEM((320, 1152), BF),
            pltpu.VMEM((64, 8, 640), F32),
            pltpu.VMEM((384, 256), BF),
            pltpu.VMEM((7, 64, 512), BF),
            pltpu.VMEM((64, 64, 128), BF),
            pltpu.VMEM((512, 512), BF),
            pltpu.VMEM((512, 512), BF),
            pltpu.VMEM((64, 16, 640), BF),
            pltpu.VMEM((64, 8, 512), F32),
            pltpu.VMEM((7, 512, 512), BF),
            pltpu.VMEM((512, 512), F32),
            pltpu.VMEM((512, 640), BF),
            pltpu.VMEM((512, 640), BF),
            pltpu.VMEM((512, 512), BF),
            pltpu.VMEM((512, 640), F32),
            pltpu.VMEM((512, 512), F32),
        ],
        cost_estimate=pl.CostEstimate(flops=2**34, bytes_accessed=2**23, transcendentals=0),
        compiler_params=pltpu.CompilerParams(vmem_limit_bytes=26 * 2**20),
    )(place, moveouts, *blocks, templates, channel_mask, whiten_taps.T, b, w)
    return reduce_lags(kept, sent).reshape(256, count)


def solution(mesh):
    in_specs = (P("chan", "tm"), P("chan", None), P(), P("tm", None), P("tm", "chan"), P("chan"))
    out_specs = P("chan", "tm")
    return jax.shard_map(shards, mesh=mesh, in_specs=in_specs, out_specs=out_specs, check_vma=False)
```

```python
import functools

import jax
import jax.numpy as jnp
from jax import lax
from jax.experimental import pallas as pl
from jax.experimental.pallas import tpu as pltpu
from jax.sharding import PartitionSpec as P

EPSILON = 1e-06
GROUP = 8
UNROLL = 8
FIRST = (2, 1, 3)
SECOND = (8, 4, 12)
PH = 8
HALO = 128
VMEM = pl.BlockSpec(memory_space=pltpu.VMEM)
SMEM = pl.BlockSpec(memory_space=pltpu.SMEM)
BF = jnp.bfloat16
F32 = jnp.float32


def lane_iota(shape):
    return lax.broadcasted_iota(jnp.int32, shape, len(shape) - 1)


def row_iota(shape):
    return lax.broadcasted_iota(jnp.int32, shape, 0)


def whiten_kernel(raw_hbm, taps_hbm, out_ref, raw_ref, taps_ref, sems):
    copies = [
        pltpu.make_async_copy(taps_hbm, taps_ref, sems.at[0]),
        pltpu.make_async_copy(raw_hbm, raw_ref, sems.at[1]),
    ]
    for copy in copies:
        copy.start()
    for copy in copies:
        copy.wait()
    taps = taps_ref[...].T
    lane = lane_iota((8, 128))
    width = raw_ref.shape[1]
    for at in range(0, raw_ref.shape[0], 16):
        halves = []
        for row in (at, at + 8):
            rows = slice(row, row + 8)
            raw = [raw_ref[rows, k : k + 128] for k in range(0, width, 128)]
            pieces = [jnp.zeros((8, 128), F32)] + raw
            acc = raw
            for m in range(1, taps.shape[1] + 1):
                tap = taps[rows, m - 1 : m]
                acc = [
                    acc[i] - tap * pltpu.roll(jnp.where(lane < 128 - m, pieces[i + 1], pieces[i]), m, 1)
                    for i in range(len(raw))
                ]
            edge = jnp.where(lane < 16, pltpu.roll(raw[-1], 16, 1), pltpu.roll(acc[0], 16, 1))
            edge = jnp.where(lane < 32, edge, 0.0)
            high = edge.astype(BF).astype(F32)
            middle = (edge - high).astype(BF).astype(F32)
            low = edge - high - middle
            edge = high + pltpu.roll(middle, 32, 1) + pltpu.roll(low, 64, 1)
            halves.append(jnp.concatenate(acc + [edge], axis=1))
        out_ref[at : at + 16, :] = jnp.concatenate(halves, axis=0).astype(BF)


def shift_left(pieces, amount, lane):
    moved = [pltpu.roll(p, jnp.where(amount == 0, 0, 128 - amount), 1) for p in pieces]
    keep = lane < 128 - amount
    return [
        jnp.where(keep, moved[i], moved[(i + 1) % len(pieces)]) for i in range(len(pieces))
    ]


def shift_static(pieces, amount, lane):
    if amount == 0:
        return pieces
    moved = [pltpu.roll(p, 128 - amount, 1) for p in pieces]
    keep = lane < 128 - amount
    return [
        jnp.where(keep, moved[i], moved[(i + 1) % len(pieces)]) for i in range(len(pieces))
    ]


def band_setup(band_ref, b_ref):
    x = lane_iota((8, 128))
    s = row_iota((8, 128))
    residue = jnp.bitwise_and(8 - s, 7)
    taps = band_ref[...].astype(F32)
    taps = jnp.concatenate([taps, jnp.zeros((1, 128 - taps.shape[1]), F32)], axis=1)
    band = jnp.broadcast_to(taps, (8, 128))
    left = jnp.where(jnp.bitwise_and(x, 7) == residue, band, 0.0).astype(BF)
    rx = row_iota((128, 128))
    rn = lane_iota((128, 128))
    right = (jnp.right_shift(rx + 16, 3) == rn).astype(F32).astype(BF)
    table = jnp.dot(left, right, preferred_element_type=F32)
    lane16 = lane_iota((16, 128))
    for v in range(PH):
        z = pltpu.roll(table, v, 0) if v else table
        z0 = pltpu.roll(z, 126, 1)
        z1 = pltpu.roll(z, 127, 1)
        upper = s <= v
        g = jnp.concatenate([jnp.where(upper, z0, z1), jnp.where(upper, z1, z)], axis=0)
        for pair in range(72):
            at = 2 * pair - 16
            turned = pltpu.roll(g, at % 128, 1) if at else g
            inside = (lane16 >= at) & (lane16 < at + 16)
            b_ref[16 * pair : 16 * pair + 16, 128 * v : 128 * v + 128] = jnp.where(
                inside, turned, 0.0
            ).astype(BF)


def setup_kernel(band_ref, tmpl_ref, b_ref, w_ref):
    count, length = tmpl_ref.shape
    wide_tmpl = tmpl_ref[...].astype(F32)
    w_ref[0:count, :] = tmpl_ref[...]
    for t in range(1, PH):
        w_ref[t * count : (t + 1) * count, :] = jnp.where(
            lane_iota((count, length)) >= t, pltpu.roll(wide_tmpl, t, 1), 0.0
        ).astype(BF)
    band_setup(band_ref, b_ref)


def spread_masks(tmpl_ref, mask_ref, ones_ref, tail_ref, m_ref):
    count, length = tmpl_ref.shape
    channels = mask_ref.shape[1]
    ri = row_iota((384, 256))
    ci = lane_iota((384, 256))
    ones_ref[...] = ((ri >= ci) & (ri < ci + 64)).astype(F32).astype(BF)
    mask = mask_ref[...].astype(F32).astype(BF)
    wide = 128 * 8
    for block in range(channels // 8):
        pick = row_iota((channels, wide)) == 8 * block + jnp.right_shift(lane_iota((channels, wide)), 7)
        spread = jnp.dot(mask, pick.astype(F32).astype(BF), preferred_element_type=F32).astype(BF)
        for k in range(8):
            m_ref[8 * block + k] = spread[:, 128 * k : 128 * k + 128]
    lanes = channels * PH
    repeat = row_iota((channels, lanes)) == jnp.right_shift(lane_iota((channels, lanes)), 3)
    spread = jnp.dot(mask, repeat.astype(F32).astype(BF), preferred_element_type=F32)
    v = jnp.bitwise_and(lane_iota((128, lanes)), PH - 1)
    j = row_iota((128, lanes))
    for t in range(1, PH):
        pick = (j == 128 - t + v) & (v < t)
        last = jnp.dot(
            tmpl_ref[:, length - 128 :], pick.astype(F32).astype(BF), preferred_element_type=F32
        )
        tail_ref[t - 1] = (last * spread).astype(BF)


def stack_kernel(place_ref, moveouts_ref, *refs):
    blocks = refs[:8]
    (tmpl_ref, mask_ref, taps_ref, b_ref, w_ref, keep_ref, *send_refs) = refs[8:17]
    (white, edges, wide, f8, w_own, ones_ref, tail_ref, m_ref, h0, h1, a_ref, s_ref, q_ref, acc,
     high_ref, low_ref, tail_rows, sums, turned) = refs[17:]
    channels, _, rows = s_ref.shape
    count, length = tmpl_ref.shape
    groups = rows // 128
    lane = lane_iota((8, 128))
    sub = row_iota((8, 128))
    spread_masks(tmpl_ref, mask_ref, ones_ref, tail_ref, m_ref)

    me = place_ref[0]
    block_time = blocks[0].shape[1] - 128
    white[:, 0:HALO] = jnp.zeros((64, HALO), BF)
    for k in range(8):
        chip = jnp.bitwise_and(jnp.right_shift(me, 1) + (k & 3), 3)
        core = jnp.bitwise_xor(jnp.bitwise_and(me, 1), k >> 2)
        when = 2 * chip + core
        at = pl.multiple_of(HALO + block_time * when, 128)
        white[:, pl.ds(at, block_time)] = blocks[k][:, 0:block_time]
        edge = blocks[k][:, block_time:].astype(F32)
        edges[when] = edge + pltpu.roll(edge, 96, 1) + pltpu.roll(edge, 64, 1)

    taps = taps_ref[...].T
    for at in range(0, 64, 16):
        fixed = []
        for row in (at, at + 8):
            rows16 = slice(row, row + 8)
            both = []
            for quad in range(2):
                start = jnp.zeros((8, 128), F32)
                before = jnp.zeros((8, 128), F32)
                for k in range(4):
                    when = 4 * quad + k
                    own = edges[when, rows16, :]
                    start = jnp.where((lane >= 32 * k + 16) & (lane < 32 * k + 32), pltpu.roll(own, 32 * k, 1) if k else own, start)
                    if when:
                        last = edges[when - 1, rows16, :]
                        before = jnp.where((lane >= 32 * k) & (lane < 32 * k + 16), pltpu.roll(last, 32 * k, 1) if k else last, before)
                for m in range(1, taps.shape[1] + 1):
                    start = start - taps[rows16, m - 1 : m] * pltpu.roll(before, m, 1)
                both.append(start)
            fixed.append(both)
        for when in range(1, 8):
            quad, k = when >> 2, when & 3
            first16 = jnp.concatenate([fixed[0][quad], fixed[1][quad]], axis=0)
            first16 = pltpu.roll(first16, (112 - 32 * k) % 128, 1)
            cols = slice(HALO + block_time * when, HALO + block_time * when + 128)
            old = white[at : at + 16, cols].astype(F32)
            white[at : at + 16, cols] = jnp.where(lane_iota((16, 128)) < 16, first16, old).astype(BF)

    tiles = 5
    for m in range(tiles):
        wide[64 * m : 64 * m + 64, :] = white[:, 1024 * m : 1024 * m + 1024 + HALO]
    for v in range(0, PH, 2):
        passed = jnp.dot(
            wide[...], b_ref[:, 128 * v : 128 * v + 256], preferred_element_type=F32
        ).astype(BF).astype(F32)
        for m in range(tiles):
            for e in range(2):
                f8[:, v + e, 128 * m : 128 * m + 128] = passed[
                    64 * m : 64 * m + 64, 128 * e : 128 * e + 128
                ]

    def align(c):
        move = moveouts_ref[c]
        move1 = jnp.right_shift(move, 3)
        move0 = jnp.bitwise_and(move, 7)
        turn = jnp.bitwise_and(8 - move0, 7)
        near = sub < 8 - move0
        whole = f8[c]
        x = [pltpu.roll(whole[:, 128 * i : 128 * i + 128], turn, 0) for i in range(5)]
        y0 = shift_left(x, move1, lane)
        y1 = shift_static(y0, 1, lane)
        y2 = shift_static(y1, 1, lane)
        a = [jnp.where(near, p, q) for p, q in zip(y0, y1)]
        nxt = [jnp.where(near, p, q) for p, q in zip(y1, y2)]
        a_ref[c] = jnp.concatenate(
            [jnp.concatenate([p, q], axis=0) for p, q in zip(a, nxt)], axis=1
        ).astype(BF)
        return jnp.concatenate(a, axis=1)

    def first(i, carry):
        for e in range(0, GROUP, 2):
            c = GROUP * i + e
            both = jnp.concatenate([align(c), align(c + 1)], axis=0)
            square = both * both
            high = square.astype(BF)
            at = pl.ds(pl.multiple_of(8 * c, 16), 16)
            high_ref[at, :] = high
            low_ref[at, :] = (square - high.astype(F32)).astype(BF)
            tail_rows[at, :] = pltpu.roll(both.astype(BF), 640 - 64, 1)[:, :rows]
        return carry

    lax.fori_loop(0, channels // GROUP, first, 0)

    for half in range(2):
        at = slice(256 * half, 256 * half + 384)
        sums[:, 256 * half : 256 * half + 256] = jnp.dot(
            high_ref[:, at], ones_ref[...], preferred_element_type=F32
        ) + jnp.dot(low_ref[:, at], ones_ref[...], preferred_element_type=F32)
    last = high_ref[:, 512:640].astype(F32) + low_ref[:, 512:640].astype(F32)
    last = jnp.sum(jnp.where(lane_iota((512, 128)) < 64, last, 0.0), axis=1, keepdims=True)
    sums[:, 512:640] = jnp.broadcast_to(last, (512, 128))

    def second(i, carry):
        for e in range(0, GROUP, 2):
            pair_scales = []
            for k in range(2):
                c = GROUP * i + e + k
                whole = sums[pl.ds(pl.multiple_of(8 * c, 8), 8), :]
                total = [whole[:, 128 * g : 128 * g + 128] for g in range(5)]
                after = shift_static(total, 1, lane)
                scales = []
                for g in range(groups):
                    suffix = total[g]
                    prefix = jnp.where(sub >= 1, pltpu.roll(after[g], 1, 0), 0.0)
                    for step in (1, 2, 4):
                        suffix = suffix + jnp.where(sub < 8 - step, pltpu.roll(suffix, 8 - step, 0), 0.0)
                        prefix = prefix + jnp.where(sub >= step, pltpu.roll(prefix, step, 0), 0.0)
                    scales.append(lax.rsqrt((suffix + prefix) / length + EPSILON))
                scales = jnp.concatenate(scales, axis=1)
                s_ref[c] = scales
                pair_scales.append(scales)
            at = pl.ds(pl.multiple_of(8 * (GROUP * i + e), 16), 16)
            tail = tail_rows[at, :].astype(F32)
            for t in range(1, PH):
                q_ref[t - 1, at, :] = jnp.concatenate(
                    [tail[8 * k : 8 * k + 8] * pair_scales[k][t : t + 1, :] for k in range(2)], axis=0
                ).astype(BF)
        return carry

    lax.fori_loop(0, channels // GROUP, second, 0)
    keep = lane_iota((16, 128))

    def build(c, h_ref):
        x = a_ref[c]
        for u in range(32):
            for g in range(groups):
                p, q = x[:, 128 * g : 128 * g + 128], x[:, 128 * g + 128 : 128 * g + 256]
                if u:
                    p = pltpu.roll(jnp.where(keep >= 2 * u, p, q), 128 - 2 * u, 1)
                h_ref[16 * u : 16 * u + 16, 128 * g : 128 * g + 128] = p

    def add_channel(h_ref, c):
        mask = m_ref[c].astype(F32)
        for nt in range(2):
            lanes = slice(256 * nt, 256 * nt + 256)
            for half in range(2):
                r = jnp.dot(
                    w_own[256 * half : 256 * half + 256, :], h_ref[:, lanes], preferred_element_type=F32
                )
                for t in range(4):
                    for g in range(2):
                        col = slice(256 * nt + 128 * g, 256 * nt + 128 * g + 128)
                        row = 4 * half + t
                        at = (slice(count * row, count * row + count), col)
                        part = r[count * t : count * t + count, 128 * g : 128 * g + 128]
                        acc[at] = acc[at] + part * (mask * s_ref[c, row : row + 1, col])

    acc[...] = jnp.zeros_like(acc)
    w_own[...] = w_ref[...]
    build(0, h0)

    def several(i, carry):
        for k in range(0, UNROLL, 2):
            c = UNROLL * i + k
            build(c + 1, h1)
            add_channel(h0, c)
            build(jnp.minimum(c + 2, channels - 1), h0)
            add_channel(h1, c + 1)
        return carry

    lax.fori_loop(0, channels // UNROLL, several, 0)

    wide_tmpl = tmpl_ref[...].astype(F32)
    power = jnp.mean(wide_tmpl * wide_tmpl, axis=1, keepdims=True)
    gain = 1.0 / (length * jnp.sqrt(power + EPSILON))
    for t in range(PH):
        at = slice(count * t, count * t + count)
        block = acc[at, :]
        if t:
            block = block + jnp.dot(tail_ref[t - 1], q_ref[t - 1], preferred_element_type=F32)
        turned[:, at] = (block * gain).T
    home = place_ref[1]
    for first_flip, ref in zip((0,) + FIRST, (keep_ref, *send_refs)):
        for p, second_flip in enumerate((0,) + SECOND):
            owner = jnp.bitwise_xor(home, first_flip ^ second_flip)
            part = turned[pl.ds(pl.multiple_of(32 * owner, 32), 32), :]
            ref[32 * p : 32 * p + 32, :] = part.astype(ref.dtype)


def gather_time(white):
    own = [white]
    for d in (1, 2, 3):
        own.append(lax.ppermute(white, "tm", [((q + 2 * d) % 8, q) for q in range(8)]))
    other = [lax.ppermute(p, "tm", [(q ^ 1, q) for q in range(8)]) for p in own]
    return own + other


def swap(value, flip):
    return lax.ppermute(value, "chan", [(i, i ^ flip) for i in range(lax.axis_size("chan"))])


def reduce_lags(kept, sent):
    total = kept
    for part, flip in zip([swap(p, f) for p, f in zip(sent, FIRST)], FIRST):
        total = total + part.astype(F32)
    narrow = total.astype(BF)
    rows = total.shape[0] // 4
    total = total[:rows]
    for k, flip in enumerate(SECOND):
        total = total + swap(narrow[rows * k + rows : rows * k + 2 * rows], flip).astype(F32)
    return total


def shards(raw_data, whiten_taps, band_taps, templates, channel_mask, moveouts):
    channels, block_time = raw_data.shape
    count, length = templates.shape
    white = pl.pallas_call(
        whiten_kernel,
        out_shape=jax.ShapeDtypeStruct((channels, block_time + 128), BF),
        in_specs=[pl.BlockSpec(memory_space=pltpu.HBM)] * 2,
        out_specs=VMEM,
        scratch_shapes=[
            pltpu.VMEM(raw_data.shape, F32),
            pltpu.VMEM(whiten_taps.T.shape, F32),
            pltpu.SemaphoreType.DMA((2,)),
        ],
        compiler_params=pltpu.CompilerParams(vmem_limit_bytes=4 * 2**20),
    )(raw_data, whiten_taps.T)
    b, w = pl.pallas_call(
        setup_kernel,
        out_shape=[
            jax.ShapeDtypeStruct((1152, 1024), BF),
            jax.ShapeDtypeStruct((512, 512), BF),
        ],
        in_specs=[VMEM] * 2,
        out_specs=[VMEM] * 2,
        cost_estimate=pl.CostEstimate(flops=2**31, bytes_accessed=2**22, transcendentals=0),
        compiler_params=pltpu.CompilerParams(vmem_limit_bytes=8 * 2**20),
    )(band_taps.reshape(1, -1), templates)
    blocks = gather_time(white)
    place = jnp.stack([lax.axis_index("tm"), lax.axis_index("chan")]).astype(jnp.int32)
    kept, *sent = pl.pallas_call(
        stack_kernel,
        out_shape=[jax.ShapeDtypeStruct((128, PH * count), F32)]
        + [jax.ShapeDtypeStruct((128, PH * count), BF)] * 3,
        in_specs=[SMEM] * 2 + [VMEM] * 13,
        out_specs=[VMEM] * 4,
        scratch_shapes=[
            pltpu.VMEM((64, HALO + 5120), BF),
            pltpu.VMEM((8, 64, 128), F32),
            pltpu.VMEM((320, 1152), BF),
            pltpu.VMEM((64, 8, 640), F32),
            pltpu.VMEM((512, 512), BF),
            pltpu.VMEM((384, 256), BF),
            pltpu.VMEM((7, 64, 512), BF),
            pltpu.VMEM((64, 64, 128), BF),
            pltpu.VMEM((512, 512), BF),
            pltpu.VMEM((512, 512), BF),
            pltpu.VMEM((64, 16, 640), BF),
            pltpu.VMEM((64, 8, 512), F32),
            pltpu.VMEM((7, 512, 512), BF),
            pltpu.VMEM((512, 512), F32),
            pltpu.VMEM((512, 640), BF),
            pltpu.VMEM((512, 640), BF),
            pltpu.VMEM((512, 512), BF),
            pltpu.VMEM((512, 640), F32),
            pltpu.VMEM((512, 512), F32),
        ],
        cost_estimate=pl.CostEstimate(flops=2**34, bytes_accessed=2**23, transcendentals=0),
        compiler_params=pltpu.CompilerParams(vmem_limit_bytes=26 * 2**20),
    )(place, moveouts, *blocks, templates, channel_mask, whiten_taps.T, b, w)
    return reduce_lags(kept, sent).reshape(256, count)


def solution(mesh):
    in_specs = (P("chan", "tm"), P("chan", None), P(), P("tm", None), P("tm", "chan"), P("chan"))
    out_specs = P("chan", "tm")
    return jax.shard_map(shards, mesh=mesh, in_specs=in_specs, out_specs=out_specs, check_vma=False)
```

```python
import functools

import jax
import jax.numpy as jnp
from jax import lax
from jax.experimental import pallas as pl
from jax.experimental.pallas import tpu as pltpu
from jax.sharding import PartitionSpec as P

EPSILON = 1e-06
GROUP = 8
UNROLL = 8
FIRST = (2, 1, 3)
SECOND = (8, 4, 12)
PH = 8
HALO = 128
VMEM = pl.BlockSpec(memory_space=pltpu.VMEM)
SMEM = pl.BlockSpec(memory_space=pltpu.SMEM)
BF = jnp.bfloat16
F32 = jnp.float32


def lane_iota(shape):
    return lax.broadcasted_iota(jnp.int32, shape, len(shape) - 1)


def row_iota(shape):
    return lax.broadcasted_iota(jnp.int32, shape, 0)


def whiten_kernel(raw_ref, taps_ref, out_ref, first_ref):
    taps = taps_ref[...].T
    lane = lane_iota((8, 128))
    rows_all, width = raw_ref.shape
    for at in range(0, rows_all, 16):
        halves = []
        for row in (at, at + 8):
            rows = slice(row, row + 8)
            raw = [raw_ref[rows, k : k + 128] for k in range(0, width, 128)]
            pieces = [jnp.zeros((8, 128), F32)] + raw
            acc = raw
            for m in range(1, taps.shape[1] + 1):
                tap = taps[rows, m - 1 : m]
                acc = [
                    acc[i] - tap * pltpu.roll(jnp.where(lane < 128 - m, pieces[i + 1], pieces[i]), m, 1)
                    for i in range(len(raw))
                ]
            first_ref[rows, :] = acc[0]
            halves.append(jnp.concatenate(acc, axis=1))
        out_ref[at : at + 16, 0:width] = jnp.concatenate(halves, axis=0).astype(BF)
    lane = lane_iota((rows_all, 128))
    edge = pltpu.roll(jnp.where(lane < 16, first_ref[...], raw_ref[:, width - 128 :]), 16, 1)
    edge = jnp.where(lane < 32, edge, 0.0)
    high = edge.astype(BF).astype(F32)
    middle = (edge - high).astype(BF).astype(F32)
    low = edge - high - middle
    edge = high + pltpu.roll(middle, 32, 1) + pltpu.roll(low, 64, 1)
    out_ref[:, width:] = edge.astype(BF)


def shift_left(pieces, amount, lane):
    moved = [pltpu.roll(p, jnp.where(amount == 0, 0, 128 - amount), 1) for p in pieces]
    keep = lane < 128 - amount
    return [
        jnp.where(keep, moved[i], moved[(i + 1) % len(pieces)]) for i in range(len(pieces))
    ]


def shift_static(pieces, amount, lane):
    if amount == 0:
        return pieces
    moved = [pltpu.roll(p, 128 - amount, 1) for p in pieces]
    keep = lane < 128 - amount
    return [
        jnp.where(keep, moved[i], moved[(i + 1) % len(pieces)]) for i in range(len(pieces))
    ]


def band_setup(band_ref, b_ref):
    x = lane_iota((8, 128))
    s = row_iota((8, 128))
    residue = jnp.bitwise_and(8 - s, 7)
    taps = band_ref[...].astype(F32)
    taps = jnp.concatenate([taps, jnp.zeros((1, 128 - taps.shape[1]), F32)], axis=1)
    band = jnp.broadcast_to(taps, (8, 128))
    left = jnp.where(jnp.bitwise_and(x, 7) == residue, band, 0.0).astype(BF)
    rx = row_iota((128, 128))
    rn = lane_iota((128, 128))
    right = (jnp.right_shift(rx + 16, 3) == rn).astype(F32).astype(BF)
    table = jnp.dot(left, right, preferred_element_type=F32)
    lane16 = lane_iota((16, 128))
    for v in range(PH):
        z = pltpu.roll(table, v, 0) if v else table
        z0 = pltpu.roll(z, 126, 1)
        z1 = pltpu.roll(z, 127, 1)
        upper = s <= v
        g = jnp.concatenate([jnp.where(upper, z0, z1), jnp.where(upper, z1, z)], axis=0)
        for pair in range(72):
            at = 2 * pair - 16
            turned = pltpu.roll(g, at % 128, 1) if at else g
            inside = (lane16 >= at) & (lane16 < at + 16)
            b_ref[16 * pair : 16 * pair + 16, 128 * v : 128 * v + 128] = jnp.where(
                inside, turned, 0.0
            ).astype(BF)


def setup_kernel(band_ref, tmpl_ref, b_ref, w_ref):
    count, length = tmpl_ref.shape
    wide_tmpl = tmpl_ref[...].astype(F32)
    w_ref[0:count, :] = tmpl_ref[...]
    for t in range(1, PH):
        w_ref[t * count : (t + 1) * count, :] = jnp.where(
            lane_iota((count, length)) >= t, pltpu.roll(wide_tmpl, t, 1), 0.0
        ).astype(BF)
    band_setup(band_ref, b_ref)


def spread_masks(tmpl_ref, mask_ref, ones_ref, tail_ref, m_ref):
    count, length = tmpl_ref.shape
    channels = mask_ref.shape[1]
    ri = row_iota((384, 256))
    ci = lane_iota((384, 256))
    ones_ref[...] = ((ri >= ci) & (ri < ci + 64)).astype(F32).astype(BF)
    mask = mask_ref[...].astype(F32).astype(BF)
    wide = 128 * 8
    for block in range(channels // 8):
        pick = row_iota((channels, wide)) == 8 * block + jnp.right_shift(lane_iota((channels, wide)), 7)
        spread = jnp.dot(mask, pick.astype(F32).astype(BF), preferred_element_type=F32).astype(BF)
        for k in range(8):
            m_ref[8 * block + k] = spread[:, 128 * k : 128 * k + 128]
    lanes = channels * PH
    repeat = row_iota((channels, lanes)) == jnp.right_shift(lane_iota((channels, lanes)), 3)
    spread = jnp.dot(mask, repeat.astype(F32).astype(BF), preferred_element_type=F32)
    v = jnp.bitwise_and(lane_iota((128, lanes)), PH - 1)
    j = row_iota((128, lanes))
    for t in range(1, PH):
        pick = (j == 128 - t + v) & (v < t)
        last = jnp.dot(
            tmpl_ref[:, length - 128 :], pick.astype(F32).astype(BF), preferred_element_type=F32
        )
        tail_ref[t - 1] = (last * spread).astype(BF)


def stack_kernel(place_ref, moveouts_ref, *refs):
    blocks = refs[:8]
    (tmpl_ref, mask_ref, taps_ref, b_ref, w_ref, keep_ref, *send_refs) = refs[8:17]
    (white, edges, wide, f8, w_own, ones_ref, tail_ref, m_ref, h0, h1, a_ref, s_ref, q_ref, acc,
     high_ref, low_ref, tail_rows, sums, turned) = refs[17:]
    channels, _, rows = s_ref.shape
    count, length = tmpl_ref.shape
    groups = rows // 128
    lane = lane_iota((8, 128))
    sub = row_iota((8, 128))
    spread_masks(tmpl_ref, mask_ref, ones_ref, tail_ref, m_ref)

    me = place_ref[0]
    block_time = blocks[0].shape[1] - 128
    white[:, 0:HALO] = jnp.zeros((64, HALO), BF)
    for k in range(8):
        chip = jnp.bitwise_and(jnp.right_shift(me, 1) + (k & 3), 3)
        core = jnp.bitwise_xor(jnp.bitwise_and(me, 1), k >> 2)
        when = 2 * chip + core
        at = pl.multiple_of(HALO + block_time * when, 128)
        white[:, pl.ds(at, block_time)] = blocks[k][:, 0:block_time]
        edge = blocks[k][:, block_time:].astype(F32)
        edges[when] = edge + pltpu.roll(edge, 96, 1) + pltpu.roll(edge, 64, 1)

    taps = taps_ref[...].T
    for at in range(0, 64, 16):
        fixed = []
        for row in (at, at + 8):
            rows16 = slice(row, row + 8)
            both = []
            for quad in range(2):
                start = jnp.zeros((8, 128), F32)
                before = jnp.zeros((8, 128), F32)
                for k in range(4):
                    when = 4 * quad + k
                    own = edges[when, rows16, :]
                    start = jnp.where((lane >= 32 * k + 16) & (lane < 32 * k + 32), pltpu.roll(own, 32 * k, 1) if k else own, start)
                    if when:
                        last = edges[when - 1, rows16, :]
                        before = jnp.where((lane >= 32 * k) & (lane < 32 * k + 16), pltpu.roll(last, 32 * k, 1) if k else last, before)
                for m in range(1, taps.shape[1] + 1):
                    start = start - taps[rows16, m - 1 : m] * pltpu.roll(before, m, 1)
                both.append(start)
            fixed.append(both)
        for when in range(1, 8):
            quad, k = when >> 2, when & 3
            first16 = jnp.concatenate([fixed[0][quad], fixed[1][quad]], axis=0)
            first16 = pltpu.roll(first16, (112 - 32 * k) % 128, 1)
            cols = slice(HALO + block_time * when, HALO + block_time * when + 128)
            old = white[at : at + 16, cols].astype(F32)
            white[at : at + 16, cols] = jnp.where(lane_iota((16, 128)) < 16, first16, old).astype(BF)

    tiles = 5
    for m in range(tiles):
        wide[64 * m : 64 * m + 64, :] = white[:, 1024 * m : 1024 * m + 1024 + HALO]
    for v in range(0, PH, 2):
        passed = jnp.dot(
            wide[...], b_ref[:, 128 * v : 128 * v + 256], preferred_element_type=F32
        ).astype(BF).astype(F32)
        for m in range(tiles):
            for e in range(2):
                f8[:, v + e, 128 * m : 128 * m + 128] = passed[
                    64 * m : 64 * m + 64, 128 * e : 128 * e + 128
                ]

    def align(c):
        move = moveouts_ref[c]
        move1 = jnp.right_shift(move, 3)
        move0 = jnp.bitwise_and(move, 7)
        turn = jnp.bitwise_and(8 - move0, 7)
        near = sub < 8 - move0
        whole = f8[c]
        x = [pltpu.roll(whole[:, 128 * i : 128 * i + 128], turn, 0) for i in range(5)]
        y0 = shift_left(x, move1, lane)
        y1 = shift_static(y0, 1, lane)
        y2 = shift_static(y1, 1, lane)
        a = [jnp.where(near, p, q) for p, q in zip(y0, y1)]
        nxt = [jnp.where(near, p, q) for p, q in zip(y1, y2)]
        a_ref[c] = jnp.concatenate(
            [jnp.concatenate([p, q], axis=0) for p, q in zip(a, nxt)], axis=1
        ).astype(BF)
        return jnp.concatenate(a, axis=1)

    def first(i, carry):
        for e in range(0, GROUP, 2):
            c = GROUP * i + e
            both = jnp.concatenate([align(c), align(c + 1)], axis=0)
            square = both * both
            high = square.astype(BF)
            at = pl.ds(pl.multiple_of(8 * c, 16), 16)
            high_ref[at, :] = high
            low_ref[at, :] = (square - high.astype(F32)).astype(BF)
            tail_rows[at, :] = pltpu.roll(both.astype(BF), 640 - 64, 1)[:, :rows]
        return carry

    lax.fori_loop(0, channels // GROUP, first, 0)

    for half in range(2):
        at = slice(256 * half, 256 * half + 384)
        sums[:, 256 * half : 256 * half + 256] = jnp.dot(
            high_ref[:, at], ones_ref[...], preferred_element_type=F32
        ) + jnp.dot(low_ref[:, at], ones_ref[...], preferred_element_type=F32)
    last = high_ref[:, 512:640].astype(F32) + low_ref[:, 512:640].astype(F32)
    last = jnp.sum(jnp.where(lane_iota((512, 128)) < 64, last, 0.0), axis=1, keepdims=True)
    sums[:, 512:640] = jnp.broadcast_to(last, (512, 128))

    def second(i, carry):
        for e in range(0, GROUP, 2):
            pair_scales = []
            for k in range(2):
                c = GROUP * i + e + k
                whole = sums[pl.ds(pl.multiple_of(8 * c, 8), 8), :]
                total = [whole[:, 128 * g : 128 * g + 128] for g in range(5)]
                after = shift_static(total, 1, lane)
                scales = []
                for g in range(groups):
                    suffix = total[g]
                    prefix = jnp.where(sub >= 1, pltpu.roll(after[g], 1, 0), 0.0)
                    for step in (1, 2, 4):
                        suffix = suffix + jnp.where(sub < 8 - step, pltpu.roll(suffix, 8 - step, 0), 0.0)
                        prefix = prefix + jnp.where(sub >= step, pltpu.roll(prefix, step, 0), 0.0)
                    scales.append(lax.rsqrt((suffix + prefix) / length + EPSILON))
                scales = jnp.concatenate(scales, axis=1)
                s_ref[c] = scales
                pair_scales.append(scales)
            at = pl.ds(pl.multiple_of(8 * (GROUP * i + e), 16), 16)
            tail = tail_rows[at, :].astype(F32)
            for t in range(1, PH):
                q_ref[t - 1, at, :] = jnp.concatenate(
                    [tail[8 * k : 8 * k + 8] * pair_scales[k][t : t + 1, :] for k in range(2)], axis=0
                ).astype(BF)
        return carry

    lax.fori_loop(0, channels // GROUP, second, 0)
    keep = lane_iota((16, 128))

    def build(c, h_ref):
        x = a_ref[c]
        for u in range(32):
            for g in range(groups):
                p, q = x[:, 128 * g : 128 * g + 128], x[:, 128 * g + 128 : 128 * g + 256]
                if u:
                    p = pltpu.roll(jnp.where(keep >= 2 * u, p, q), 128 - 2 * u, 1)
                h_ref[16 * u : 16 * u + 16, 128 * g : 128 * g + 128] = p

    def add_channel(h_ref, c):
        mask = m_ref[c].astype(F32)
        for nt in range(2):
            lanes = slice(256 * nt, 256 * nt + 256)
            for half in range(2):
                r = jnp.dot(
                    w_own[256 * half : 256 * half + 256, :], h_ref[:, lanes], preferred_element_type=F32
                )
                for t in range(4):
                    for g in range(2):
                        col = slice(256 * nt + 128 * g, 256 * nt + 128 * g + 128)
                        row = 4 * half + t
                        at = (slice(count * row, count * row + count), col)
                        part = r[count * t : count * t + count, 128 * g : 128 * g + 128]
                        acc[at] = acc[at] + part * (mask * s_ref[c, row : row + 1, col])

    acc[...] = jnp.zeros_like(acc)
    w_own[...] = w_ref[...]
    build(0, h0)

    def several(i, carry):
        for k in range(0, UNROLL, 2):
            c = UNROLL * i + k
            build(c + 1, h1)
            add_channel(h0, c)
            build(jnp.minimum(c + 2, channels - 1), h0)
            add_channel(h1, c + 1)
        return carry

    lax.fori_loop(0, channels // UNROLL, several, 0)

    wide_tmpl = tmpl_ref[...].astype(F32)
    power = jnp.mean(wide_tmpl * wide_tmpl, axis=1, keepdims=True)
    gain = 1.0 / (length * jnp.sqrt(power + EPSILON))
    for t in range(PH):
        at = slice(count * t, count * t + count)
        block = acc[at, :]
        if t:
            block = block + jnp.dot(tail_ref[t - 1], q_ref[t - 1], preferred_element_type=F32)
        turned[:, at] = (block * gain).T
    home = place_ref[1]
    for first_flip, ref in zip((0,) + FIRST, (keep_ref, *send_refs)):
        for p, second_flip in enumerate((0,) + SECOND):
            owner = jnp.bitwise_xor(home, first_flip ^ second_flip)
            part = turned[pl.ds(pl.multiple_of(32 * owner, 32), 32), :]
            ref[32 * p : 32 * p + 32, :] = part.astype(ref.dtype)


def gather_time(white):
    own = [white]
    for d in (1, 2, 3):
        own.append(lax.ppermute(white, "tm", [((q + 2 * d) % 8, q) for q in range(8)]))
    other = [lax.ppermute(p, "tm", [(q ^ 1, q) for q in range(8)]) for p in own]
    return own + other


def swap(value, flip):
    return lax.ppermute(value, "chan", [(i, i ^ flip) for i in range(lax.axis_size("chan"))])


def reduce_lags(kept, sent):
    total = kept
    for part, flip in zip([swap(p, f) for p, f in zip(sent, FIRST)], FIRST):
        total = total + part.astype(F32)
    narrow = total.astype(BF)
    rows = total.shape[0] // 4
    total = total[:rows]
    for k, flip in enumerate(SECOND):
        total = total + swap(narrow[rows * k + rows : rows * k + 2 * rows], flip).astype(F32)
    return total


def shards(raw_data, whiten_taps, band_taps, templates, channel_mask, moveouts):
    channels, block_time = raw_data.shape
    count, length = templates.shape
    white = pl.pallas_call(
        whiten_kernel,
        out_shape=jax.ShapeDtypeStruct((channels, block_time + 128), BF),
        in_specs=[VMEM] * 2,
        out_specs=VMEM,
        scratch_shapes=[pltpu.VMEM((channels, 128), F32)],
        compiler_params=pltpu.CompilerParams(vmem_limit_bytes=4 * 2**20),
    )(raw_data, whiten_taps.T)
    b, w = pl.pallas_call(
        setup_kernel,
        out_shape=[
            jax.ShapeDtypeStruct((1152, 1024), BF),
            jax.ShapeDtypeStruct((512, 512), BF),
        ],
        in_specs=[VMEM] * 2,
        out_specs=[VMEM] * 2,
        cost_estimate=pl.CostEstimate(flops=2**31, bytes_accessed=2**22, transcendentals=0),
        compiler_params=pltpu.CompilerParams(vmem_limit_bytes=8 * 2**20),
    )(band_taps.reshape(1, -1), templates)
    blocks = gather_time(white)
    place = jnp.stack([lax.axis_index("tm"), lax.axis_index("chan")]).astype(jnp.int32)
    kept, *sent = pl.pallas_call(
        stack_kernel,
        out_shape=[jax.ShapeDtypeStruct((128, PH * count), F32)]
        + [jax.ShapeDtypeStruct((128, PH * count), BF)] * 3,
        in_specs=[SMEM] * 2 + [VMEM] * 13,
        out_specs=[VMEM] * 4,
        scratch_shapes=[
            pltpu.VMEM((64, HALO + 5120), BF),
            pltpu.VMEM((8, 64, 128), F32),
            pltpu.VMEM((320, 1152), BF),
            pltpu.VMEM((64, 8, 640), F32),
            pltpu.VMEM((512, 512), BF),
            pltpu.VMEM((384, 256), BF),
            pltpu.VMEM((7, 64, 512), BF),
            pltpu.VMEM((64, 64, 128), BF),
            pltpu.VMEM((512, 512), BF),
            pltpu.VMEM((512, 512), BF),
            pltpu.VMEM((64, 16, 640), BF),
            pltpu.VMEM((64, 8, 512), F32),
            pltpu.VMEM((7, 512, 512), BF),
            pltpu.VMEM((512, 512), F32),
            pltpu.VMEM((512, 640), BF),
            pltpu.VMEM((512, 640), BF),
            pltpu.VMEM((512, 512), BF),
            pltpu.VMEM((512, 640), F32),
            pltpu.VMEM((512, 512), F32),
        ],
        cost_estimate=pl.CostEstimate(flops=2**34, bytes_accessed=2**23, transcendentals=0),
        compiler_params=pltpu.CompilerParams(vmem_limit_bytes=26 * 2**20),
    )(place, moveouts, *blocks, templates, channel_mask, whiten_taps.T, b, w)
    return reduce_lags(kept, sent).reshape(256, count)


def solution(mesh):
    in_specs = (P("chan", "tm"), P("chan", None), P(), P("tm", None), P("tm", "chan"), P("chan"))
    out_specs = P("chan", "tm")
    return jax.shard_map(shards, mesh=mesh, in_specs=in_specs, out_specs=out_specs, check_vma=False)
```

```python
import functools

import jax
import jax.numpy as jnp
from jax import lax
from jax.experimental import pallas as pl
from jax.experimental.pallas import tpu as pltpu
from jax.sharding import PartitionSpec as P

EPSILON = 1e-06
GROUP = 8
UNROLL = 8
FIRST = (2, 1, 3)
SECOND = (8, 4, 12)
PH = 8
HALO = 128
VMEM = pl.BlockSpec(memory_space=pltpu.VMEM)
SMEM = pl.BlockSpec(memory_space=pltpu.SMEM)
BF = jnp.bfloat16
F32 = jnp.float32


def lane_iota(shape):
    return lax.broadcasted_iota(jnp.int32, shape, len(shape) - 1)


def row_iota(shape):
    return lax.broadcasted_iota(jnp.int32, shape, 0)


def whiten_kernel(raw_ref, taps_ref, out_ref, first_ref):
    taps = taps_ref[...].T
    lane = lane_iota((8, 128))
    rows_all, width = raw_ref.shape
    for at in range(0, rows_all, 16):
        halves = []
        for row in (at, at + 8):
            rows = slice(row, row + 8)
            raw = [raw_ref[rows, k : k + 128] for k in range(0, width, 128)]
            pieces = [jnp.zeros((8, 128), F32)] + raw
            acc = raw
            for m in range(1, taps.shape[1] + 1):
                tap = taps[rows, m - 1 : m]
                acc = [
                    acc[i] - tap * pltpu.roll(jnp.where(lane < 128 - m, pieces[i + 1], pieces[i]), m, 1)
                    for i in range(len(raw))
                ]
            first_ref[rows, :] = acc[0]
            halves.append(jnp.concatenate(acc, axis=1))
        out_ref[at : at + 16, 0:width] = jnp.concatenate(halves, axis=0).astype(BF)
    lane = lane_iota((rows_all, 128))
    edge = pltpu.roll(jnp.where(lane < 16, first_ref[...], raw_ref[:, width - 128 :]), 16, 1)
    edge = jnp.where(lane < 32, edge, 0.0)
    high = edge.astype(BF).astype(F32)
    middle = (edge - high).astype(BF).astype(F32)
    low = edge - high - middle
    edge = high + pltpu.roll(middle, 32, 1) + pltpu.roll(low, 64, 1)
    out_ref[:, width:] = edge.astype(BF)


def shift_left(pieces, amount, lane):
    moved = [pltpu.roll(p, jnp.where(amount == 0, 0, 128 - amount), 1) for p in pieces]
    keep = lane < 128 - amount
    return [
        jnp.where(keep, moved[i], moved[(i + 1) % len(pieces)]) for i in range(len(pieces))
    ]


def shift_static(pieces, amount, lane):
    if amount == 0:
        return pieces
    moved = [pltpu.roll(p, 128 - amount, 1) for p in pieces]
    keep = lane < 128 - amount
    return [
        jnp.where(keep, moved[i], moved[(i + 1) % len(pieces)]) for i in range(len(pieces))
    ]


def band_setup(band_ref, b_ref):
    x = lane_iota((8, 128))
    s = row_iota((8, 128))
    residue = jnp.bitwise_and(8 - s, 7)
    taps = band_ref[...].astype(F32)
    taps = jnp.concatenate([taps, jnp.zeros((1, 128 - taps.shape[1]), F32)], axis=1)
    band = jnp.broadcast_to(taps, (8, 128))
    left = jnp.where(jnp.bitwise_and(x, 7) == residue, band, 0.0).astype(BF)
    rx = row_iota((128, 128))
    rn = lane_iota((128, 128))
    right = (jnp.right_shift(rx + 16, 3) == rn).astype(F32).astype(BF)
    table = jnp.dot(left, right, preferred_element_type=F32)
    lane16 = lane_iota((16, 128))
    for v in range(PH):
        z = pltpu.roll(table, v, 0) if v else table
        z0 = pltpu.roll(z, 126, 1)
        z1 = pltpu.roll(z, 127, 1)
        upper = s <= v
        g = jnp.concatenate([jnp.where(upper, z0, z1), jnp.where(upper, z1, z)], axis=0)
        for pair in range(72):
            at = 2 * pair - 16
            turned = pltpu.roll(g, at % 128, 1) if at else g
            inside = (lane16 >= at) & (lane16 < at + 16)
            b_ref[16 * pair : 16 * pair + 16, 128 * v : 128 * v + 128] = jnp.where(
                inside, turned, 0.0
            ).astype(BF)


def setup_kernel(band_ref, tmpl_ref, b_ref, w_ref):
    count, length = tmpl_ref.shape
    wide_tmpl = tmpl_ref[...].astype(F32)
    w_ref[0:count, :] = tmpl_ref[...]
    for t in range(1, PH):
        w_ref[t * count : (t + 1) * count, :] = jnp.where(
            lane_iota((count, length)) >= t, pltpu.roll(wide_tmpl, t, 1), 0.0
        ).astype(BF)
    band_setup(band_ref, b_ref)


def spread_masks(tmpl_ref, mask_ref, ones_ref, tail_ref, m_ref):
    count, length = tmpl_ref.shape
    channels = mask_ref.shape[1]
    ri = row_iota((384, 256))
    ci = lane_iota((384, 256))
    ones_ref[...] = ((ri >= ci) & (ri < ci + 64)).astype(F32).astype(BF)
    mask = mask_ref[...].astype(F32).astype(BF)
    wide = 128 * 8
    for block in range(channels // 8):
        pick = row_iota((channels, wide)) == 8 * block + jnp.right_shift(lane_iota((channels, wide)), 7)
        spread = jnp.dot(mask, pick.astype(F32).astype(BF), preferred_element_type=F32).astype(BF)
        for k in range(8):
            m_ref[8 * block + k] = spread[:, 128 * k : 128 * k + 128]
    lanes = channels * PH
    repeat = row_iota((channels, lanes)) == jnp.right_shift(lane_iota((channels, lanes)), 3)
    spread = jnp.dot(mask, repeat.astype(F32).astype(BF), preferred_element_type=F32)
    v = jnp.bitwise_and(lane_iota((128, lanes)), PH - 1)
    j = row_iota((128, lanes))
    for t in range(1, PH):
        pick = (j == 128 - t + v) & (v < t)
        last = jnp.dot(
            tmpl_ref[:, length - 128 :], pick.astype(F32).astype(BF), preferred_element_type=F32
        )
        tail_ref[t - 1] = (last * spread).astype(BF)


def stack_kernel(place_ref, moveouts_ref, *refs):
    blocks = refs[:8]
    (tmpl_ref, mask_ref, taps_ref, b_ref, w_ref, keep_ref, *send_refs) = refs[8:17]
    (white, edges, wide, f8, w_own, ones_ref, tail_ref, m_ref, h0, h1, a_ref, s_ref, q_ref, acc,
     high_ref, low_ref, tail_rows, sums, turned) = refs[17:]
    channels, _, rows = s_ref.shape
    count, length = tmpl_ref.shape
    groups = rows // 128
    lane = lane_iota((8, 128))
    sub = row_iota((8, 128))
    spread_masks(tmpl_ref, mask_ref, ones_ref, tail_ref, m_ref)

    me = place_ref[0]
    block_time = blocks[0].shape[1] - 128
    white[:, 0:HALO] = jnp.zeros((64, HALO), BF)
    for k in range(8):
        chip = jnp.bitwise_and(jnp.right_shift(me, 1) + (k & 3), 3)
        core = jnp.bitwise_xor(jnp.bitwise_and(me, 1), k >> 2)
        when = 2 * chip + core
        at = pl.multiple_of(HALO + block_time * when, 128)
        white[:, pl.ds(at, block_time)] = blocks[k][:, 0:block_time]
        edge = blocks[k][:, block_time:].astype(F32)
        edges[when] = edge + pltpu.roll(edge, 96, 1) + pltpu.roll(edge, 64, 1)

    taps = taps_ref[...].T
    for at in range(0, 64, 16):
        fixed = []
        for row in (at, at + 8):
            rows16 = slice(row, row + 8)
            both = []
            for quad in range(2):
                start = jnp.zeros((8, 128), F32)
                before = jnp.zeros((8, 128), F32)
                for k in range(4):
                    when = 4 * quad + k
                    own = edges[when, rows16, :]
                    start = jnp.where((lane >= 32 * k + 16) & (lane < 32 * k + 32), pltpu.roll(own, 32 * k, 1) if k else own, start)
                    if when:
                        last = edges[when - 1, rows16, :]
                        before = jnp.where((lane >= 32 * k) & (lane < 32 * k + 16), pltpu.roll(last, 32 * k, 1) if k else last, before)
                for m in range(1, taps.shape[1] + 1):
                    start = start - taps[rows16, m - 1 : m] * pltpu.roll(before, m, 1)
                both.append(start)
            fixed.append(both)
        for when in range(1, 8):
            quad, k = when >> 2, when & 3
            first16 = jnp.concatenate([fixed[0][quad], fixed[1][quad]], axis=0)
            first16 = pltpu.roll(first16, (112 - 32 * k) % 128, 1)
            cols = slice(HALO + block_time * when, HALO + block_time * when + 128)
            old = white[at : at + 16, cols].astype(F32)
            white[at : at + 16, cols] = jnp.where(lane_iota((16, 128)) < 16, first16, old).astype(BF)

    tiles = 5
    for m in range(tiles):
        wide[64 * m : 64 * m + 64, :] = white[:, 1024 * m : 1024 * m + 1024 + HALO]
    for v in range(0, PH, 2):
        passed = jnp.dot(
            wide[...], b_ref[:, 128 * v : 128 * v + 256], preferred_element_type=F32
        ).astype(BF).astype(F32)
        for m in range(tiles):
            for e in range(2):
                f8[:, v + e, 128 * m : 128 * m + 128] = passed[
                    64 * m : 64 * m + 64, 128 * e : 128 * e + 128
                ]

    lane16 = lane_iota((16, 128))

    def align(first_channel):
        base, nears = [], []
        for c in (first_channel, first_channel + 1):
            move = moveouts_ref[c]
            move1 = jnp.right_shift(move, 3)
            move0 = jnp.bitwise_and(move, 7)
            turn = jnp.bitwise_and(8 - move0, 7)
            nears.append(sub < 8 - move0)
            whole = f8[c]
            x = [pltpu.roll(whole[:, 128 * i : 128 * i + 128], turn, 0) for i in range(5)]
            base.append(shift_left(x, move1, lane))
        y0 = [jnp.concatenate([p, q], axis=0) for p, q in zip(*base)]
        y1 = shift_static([p.astype(BF) for p in y0], 1, lane16)
        y2 = [p.astype(F32) for p in shift_static(y1, 1, lane16)]
        y1 = [p.astype(F32) for p in y1]
        both = []
        for k in range(2):
            rows8 = slice(8 * k, 8 * k + 8)
            a = [jnp.where(nears[k], p, q[rows8]) for p, q in zip(base[k], y1)]
            nxt = [jnp.where(nears[k], p[rows8], q[rows8]) for p, q in zip(y1, y2)]
            a_ref[first_channel + k] = jnp.concatenate(
                [jnp.concatenate([p, q], axis=0) for p, q in zip(a, nxt)], axis=1
            ).astype(BF)
            both.append(jnp.concatenate(a, axis=1))
        return jnp.concatenate(both, axis=0)

    def first(i, carry):
        for e in range(0, GROUP, 2):
            c = GROUP * i + e
            both = align(c)
            square = both * both
            high = square.astype(BF)
            at = pl.ds(pl.multiple_of(8 * c, 16), 16)
            high_ref[at, :] = high
            low_ref[at, :] = (square - high.astype(F32)).astype(BF)
            tail_rows[at, :] = pltpu.roll(both.astype(BF), 640 - 64, 1)[:, :rows]
        return carry

    lax.fori_loop(0, channels // GROUP, first, 0)

    for half in range(2):
        at = slice(256 * half, 256 * half + 384)
        sums[:, 256 * half : 256 * half + 256] = jnp.dot(
            high_ref[:, at], ones_ref[...], preferred_element_type=F32
        ) + jnp.dot(low_ref[:, at], ones_ref[...], preferred_element_type=F32)
    last = high_ref[:, 512:640].astype(F32) + low_ref[:, 512:640].astype(F32)
    last = jnp.sum(jnp.where(lane_iota((512, 128)) < 64, last, 0.0), axis=1, keepdims=True)
    sums[:, 512:640] = jnp.broadcast_to(last, (512, 128))

    def second(i, carry):
        for e in range(0, GROUP, 2):
            pair_scales = []
            for k in range(2):
                c = GROUP * i + e + k
                whole = sums[pl.ds(pl.multiple_of(8 * c, 8), 8), :]
                total = [whole[:, 128 * g : 128 * g + 128] for g in range(5)]
                after = shift_static(total, 1, lane)
                scales = []
                for g in range(groups):
                    suffix = total[g]
                    prefix = jnp.where(sub >= 1, pltpu.roll(after[g], 1, 0), 0.0)
                    for step in (1, 2, 4):
                        suffix = suffix + jnp.where(sub < 8 - step, pltpu.roll(suffix, 8 - step, 0), 0.0)
                        prefix = prefix + jnp.where(sub >= step, pltpu.roll(prefix, step, 0), 0.0)
                    scales.append(lax.rsqrt((suffix + prefix) / length + EPSILON))
                scales = jnp.concatenate(scales, axis=1)
                s_ref[c] = scales
                pair_scales.append(scales)
            at = pl.ds(pl.multiple_of(8 * (GROUP * i + e), 16), 16)
            tail = tail_rows[at, :].astype(F32)
            for t in range(1, PH):
                q_ref[t - 1, at, :] = jnp.concatenate(
                    [tail[8 * k : 8 * k + 8] * pair_scales[k][t : t + 1, :] for k in range(2)], axis=0
                ).astype(BF)
        return carry

    lax.fori_loop(0, channels // GROUP, second, 0)
    keep = lane_iota((16, 128))

    def build(c, h_ref):
        x = a_ref[c]
        for u in range(32):
            for g in range(groups):
                p, q = x[:, 128 * g : 128 * g + 128], x[:, 128 * g + 128 : 128 * g + 256]
                if u:
                    p = pltpu.roll(jnp.where(keep >= 2 * u, p, q), 128 - 2 * u, 1)
                h_ref[16 * u : 16 * u + 16, 128 * g : 128 * g + 128] = p

    def add_channel(h_ref, c):
        mask = m_ref[c].astype(F32)
        for nt in range(2):
            lanes = slice(256 * nt, 256 * nt + 256)
            for half in range(2):
                r = jnp.dot(
                    w_own[256 * half : 256 * half + 256, :], h_ref[:, lanes], preferred_element_type=F32
                )
                for t in range(4):
                    for g in range(2):
                        col = slice(256 * nt + 128 * g, 256 * nt + 128 * g + 128)
                        row = 4 * half + t
                        at = (slice(count * row, count * row + count), col)
                        part = r[count * t : count * t + count, 128 * g : 128 * g + 128]
                        acc[at] = acc[at] + part * (mask * s_ref[c, row : row + 1, col])

    acc[...] = jnp.zeros_like(acc)
    w_own[...] = w_ref[...]
    build(0, h0)

    def several(i, carry):
        for k in range(0, UNROLL, 2):
            c = UNROLL * i + k
            build(c + 1, h1)
            add_channel(h0, c)
            build(jnp.minimum(c + 2, channels - 1), h0)
            add_channel(h1, c + 1)
        return carry

    lax.fori_loop(0, channels // UNROLL, several, 0)

    wide_tmpl = tmpl_ref[...].astype(F32)
    power = jnp.mean(wide_tmpl * wide_tmpl, axis=1, keepdims=True)
    gain = 1.0 / (length * jnp.sqrt(power + EPSILON))
    for t in range(PH):
        at = slice(count * t, count * t + count)
        block = acc[at, :]
        if t:
            block = block + jnp.dot(tail_ref[t - 1], q_ref[t - 1], preferred_element_type=F32)
        turned[:, at] = (block * gain).T
    home = place_ref[1]
    for first_flip, ref in zip((0,) + FIRST, (keep_ref, *send_refs)):
        for p, second_flip in enumerate((0,) + SECOND):
            owner = jnp.bitwise_xor(home, first_flip ^ second_flip)
            part = turned[pl.ds(pl.multiple_of(32 * owner, 32), 32), :]
            ref[32 * p : 32 * p + 32, :] = part.astype(ref.dtype)


def gather_time(white):
    own = [white]
    for d in (1, 2, 3):
        own.append(lax.ppermute(white, "tm", [((q + 2 * d) % 8, q) for q in range(8)]))
    other = [lax.ppermute(p, "tm", [(q ^ 1, q) for q in range(8)]) for p in own]
    return own + other


def swap(value, flip):
    return lax.ppermute(value, "chan", [(i, i ^ flip) for i in range(lax.axis_size("chan"))])


def reduce_lags(kept, sent):
    total = kept
    for part, flip in zip([swap(p, f) for p, f in zip(sent, FIRST)], FIRST):
        total = total + part.astype(F32)
    narrow = total.astype(BF)
    rows = total.shape[0] // 4
    total = total[:rows]
    for k, flip in enumerate(SECOND):
        total = total + swap(narrow[rows * k + rows : rows * k + 2 * rows], flip).astype(F32)
    return total


def shards(raw_data, whiten_taps, band_taps, templates, channel_mask, moveouts):
    channels, block_time = raw_data.shape
    count, length = templates.shape
    white = pl.pallas_call(
        whiten_kernel,
        out_shape=jax.ShapeDtypeStruct((channels, block_time + 128), BF),
        in_specs=[VMEM] * 2,
        out_specs=VMEM,
        scratch_shapes=[pltpu.VMEM((channels, 128), F32)],
        compiler_params=pltpu.CompilerParams(vmem_limit_bytes=4 * 2**20),
    )(raw_data, whiten_taps.T)
    b, w = pl.pallas_call(
        setup_kernel,
        out_shape=[
            jax.ShapeDtypeStruct((1152, 1024), BF),
            jax.ShapeDtypeStruct((512, 512), BF),
        ],
        in_specs=[VMEM] * 2,
        out_specs=[VMEM] * 2,
        cost_estimate=pl.CostEstimate(flops=2**31, bytes_accessed=2**22, transcendentals=0),
        compiler_params=pltpu.CompilerParams(vmem_limit_bytes=8 * 2**20),
    )(band_taps.reshape(1, -1), templates)
    blocks = gather_time(white)
    place = jnp.stack([lax.axis_index("tm"), lax.axis_index("chan")]).astype(jnp.int32)
    kept, *sent = pl.pallas_call(
        stack_kernel,
        out_shape=[jax.ShapeDtypeStruct((128, PH * count), F32)]
        + [jax.ShapeDtypeStruct((128, PH * count), BF)] * 3,
        in_specs=[SMEM] * 2 + [VMEM] * 13,
        out_specs=[VMEM] * 4,
        scratch_shapes=[
            pltpu.VMEM((64, HALO + 5120), BF),
            pltpu.VMEM((8, 64, 128), F32),
            pltpu.VMEM((320, 1152), BF),
            pltpu.VMEM((64, 8, 640), F32),
            pltpu.VMEM((512, 512), BF),
            pltpu.VMEM((384, 256), BF),
            pltpu.VMEM((7, 64, 512), BF),
            pltpu.VMEM((64, 64, 128), BF),
            pltpu.VMEM((512, 512), BF),
            pltpu.VMEM((512, 512), BF),
            pltpu.VMEM((64, 16, 640), BF),
            pltpu.VMEM((64, 8, 512), F32),
            pltpu.VMEM((7, 512, 512), BF),
            pltpu.VMEM((512, 512), F32),
            pltpu.VMEM((512, 640), BF),
            pltpu.VMEM((512, 640), BF),
            pltpu.VMEM((512, 512), BF),
            pltpu.VMEM((512, 640), F32),
            pltpu.VMEM((512, 512), F32),
        ],
        cost_estimate=pl.CostEstimate(flops=2**34, bytes_accessed=2**23, transcendentals=0),
        compiler_params=pltpu.CompilerParams(vmem_limit_bytes=26 * 2**20),
    )(place, moveouts, *blocks, templates, channel_mask, whiten_taps.T, b, w)
    return reduce_lags(kept, sent).reshape(256, count)


def solution(mesh):
    in_specs = (P("chan", "tm"), P("chan", None), P(), P("tm", None), P("tm", "chan"), P("chan"))
    out_specs = P("chan", "tm")
    return jax.shard_map(shards, mesh=mesh, in_specs=in_specs, out_specs=out_specs, check_vma=False)
```

```python
import functools

import jax
import jax.numpy as jnp
from jax import lax
from jax.experimental import pallas as pl
from jax.experimental.pallas import tpu as pltpu
from jax.sharding import PartitionSpec as P

EPSILON = 1e-06
GROUP = 8
UNROLL = 8
FIRST = (1, 3, 2)
SECOND = (8, 4, 12)
PH = 8
HALO = 128
VMEM = pl.BlockSpec(memory_space=pltpu.VMEM)
SMEM = pl.BlockSpec(memory_space=pltpu.SMEM)
BF = jnp.bfloat16
F32 = jnp.float32


def lane_iota(shape):
    return lax.broadcasted_iota(jnp.int32, shape, len(shape) - 1)


def row_iota(shape):
    return lax.broadcasted_iota(jnp.int32, shape, 0)


def whiten_kernel(raw_ref, taps_ref, out_ref, first_ref):
    taps = taps_ref[...].T
    lane = lane_iota((8, 128))
    rows_all, width = raw_ref.shape
    for at in range(0, rows_all, 16):
        halves = []
        for row in (at, at + 8):
            rows = slice(row, row + 8)
            raw = [raw_ref[rows, k : k + 128] for k in range(0, width, 128)]
            pieces = [jnp.zeros((8, 128), F32)] + raw
            acc = raw
            for m in range(1, taps.shape[1] + 1):
                tap = taps[rows, m - 1 : m]
                acc = [
                    acc[i] - tap * pltpu.roll(jnp.where(lane < 128 - m, pieces[i + 1], pieces[i]), m, 1)
                    for i in range(len(raw))
                ]
            first_ref[rows, :] = acc[0]
            halves.append(jnp.concatenate(acc, axis=1))
        out_ref[at : at + 16, 0:width] = jnp.concatenate(halves, axis=0).astype(BF)
    lane = lane_iota((rows_all, 128))
    edge = pltpu.roll(jnp.where(lane < 16, first_ref[...], raw_ref[:, width - 128 :]), 16, 1)
    edge = jnp.where(lane < 32, edge, 0.0)
    high = edge.astype(BF).astype(F32)
    middle = (edge - high).astype(BF).astype(F32)
    low = edge - high - middle
    edge = high + pltpu.roll(middle, 32, 1) + pltpu.roll(low, 64, 1)
    out_ref[:, width:] = edge.astype(BF)


def shift_left(pieces, amount, lane):
    moved = [pltpu.roll(p, jnp.where(amount == 0, 0, 128 - amount), 1) for p in pieces]
    keep = lane < 128 - amount
    return [
        jnp.where(keep, moved[i], moved[(i + 1) % len(pieces)]) for i in range(len(pieces))
    ]


def shift_static(pieces, amount, lane):
    if amount == 0:
        return pieces
    moved = [pltpu.roll(p, 128 - amount, 1) for p in pieces]
    keep = lane < 128 - amount
    return [
        jnp.where(keep, moved[i], moved[(i + 1) % len(pieces)]) for i in range(len(pieces))
    ]


def band_setup(band_ref, b_ref):
    x = lane_iota((8, 128))
    s = row_iota((8, 128))
    residue = jnp.bitwise_and(8 - s, 7)
    taps = band_ref[...].astype(F32)
    taps = jnp.concatenate([taps, jnp.zeros((1, 128 - taps.shape[1]), F32)], axis=1)
    band = jnp.broadcast_to(taps, (8, 128))
    left = jnp.where(jnp.bitwise_and(x, 7) == residue, band, 0.0).astype(BF)
    rx = row_iota((128, 128))
    rn = lane_iota((128, 128))
    right = (jnp.right_shift(rx + 16, 3) == rn).astype(F32).astype(BF)
    table = jnp.dot(left, right, preferred_element_type=F32)
    lane16 = lane_iota((16, 128))
    for v in range(PH):
        z = pltpu.roll(table, v, 0) if v else table
        z0 = pltpu.roll(z, 126, 1)
        z1 = pltpu.roll(z, 127, 1)
        upper = s <= v
        g = jnp.concatenate([jnp.where(upper, z0, z1), jnp.where(upper, z1, z)], axis=0)
        for pair in range(72):
            at = 2 * pair - 16
            turned = pltpu.roll(g, at % 128, 1) if at else g
            inside = (lane16 >= at) & (lane16 < at + 16)
            b_ref[16 * pair : 16 * pair + 16, 128 * v : 128 * v + 128] = jnp.where(
                inside, turned, 0.0
            ).astype(BF)


def setup_kernel(band_ref, tmpl_ref, b_ref, w_ref):
    count, length = tmpl_ref.shape
    wide_tmpl = tmpl_ref[...].astype(F32)
    w_ref[0:count, :] = tmpl_ref[...]
    for t in range(1, PH):
        w_ref[t * count : (t + 1) * count, :] = jnp.where(
            lane_iota((count, length)) >= t, pltpu.roll(wide_tmpl, t, 1), 0.0
        ).astype(BF)
    band_setup(band_ref, b_ref)


def spread_masks(tmpl_ref, mask_ref, ones_ref, tail_ref, m_ref):
    count, length = tmpl_ref.shape
    channels = mask_ref.shape[1]
    ri = row_iota((384, 256))
    ci = lane_iota((384, 256))
    ones_ref[...] = ((ri >= ci) & (ri < ci + 64)).astype(F32).astype(BF)
    mask = mask_ref[...].astype(F32).astype(BF)
    wide = 128 * 8
    for block in range(channels // 8):
        pick = row_iota((channels, wide)) == 8 * block + jnp.right_shift(lane_iota((channels, wide)), 7)
        spread = jnp.dot(mask, pick.astype(F32).astype(BF), preferred_element_type=F32).astype(BF)
        for k in range(8):
            m_ref[8 * block + k] = spread[:, 128 * k : 128 * k + 128]
    lanes = channels * PH
    repeat = row_iota((channels, lanes)) == jnp.right_shift(lane_iota((channels, lanes)), 3)
    spread = jnp.dot(mask, repeat.astype(F32).astype(BF), preferred_element_type=F32)
    v = jnp.bitwise_and(lane_iota((128, lanes)), PH - 1)
    j = row_iota((128, lanes))
    for t in range(1, PH):
        pick = (j == 128 - t + v) & (v < t)
        last = jnp.dot(
            tmpl_ref[:, length - 128 :], pick.astype(F32).astype(BF), preferred_element_type=F32
        )
        tail_ref[t - 1] = (last * spread).astype(BF)


def stack_kernel(place_ref, moveouts_ref, *refs):
    blocks = refs[:8]
    (tmpl_ref, mask_ref, taps_ref, b_ref, w_ref, keep_ref, *send_refs) = refs[8:17]
    (white, edges, wide, f8, w_own, ones_ref, tail_ref, m_ref, h0, h1, a_ref, s_ref, q_ref, acc,
     high_ref, low_ref, tail_rows, sums, turned) = refs[17:]
    channels, _, rows = s_ref.shape
    count, length = tmpl_ref.shape
    groups = rows // 128
    lane = lane_iota((8, 128))
    sub = row_iota((8, 128))
    spread_masks(tmpl_ref, mask_ref, ones_ref, tail_ref, m_ref)

    me = place_ref[0]
    block_time = blocks[0].shape[1] - 128
    white[:, 0:HALO] = jnp.zeros((64, HALO), BF)
    for k in range(8):
        chip = jnp.bitwise_and(jnp.right_shift(me, 1) + (k & 3), 3)
        core = jnp.bitwise_xor(jnp.bitwise_and(me, 1), k >> 2)
        when = 2 * chip + core
        at = pl.multiple_of(HALO + block_time * when, 128)
        white[:, pl.ds(at, block_time)] = blocks[k][:, 0:block_time]
        edge = blocks[k][:, block_time:].astype(F32)
        edges[when] = edge + pltpu.roll(edge, 96, 1) + pltpu.roll(edge, 64, 1)

    taps = taps_ref[...].T
    for at in range(0, 64, 16):
        fixed = []
        for row in (at, at + 8):
            rows16 = slice(row, row + 8)
            both = []
            for quad in range(2):
                start = jnp.zeros((8, 128), F32)
                before = jnp.zeros((8, 128), F32)
                for k in range(4):
                    when = 4 * quad + k
                    own = edges[when, rows16, :]
                    start = jnp.where((lane >= 32 * k + 16) & (lane < 32 * k + 32), pltpu.roll(own, 32 * k, 1) if k else own, start)
                    if when:
                        last = edges[when - 1, rows16, :]
                        before = jnp.where((lane >= 32 * k) & (lane < 32 * k + 16), pltpu.roll(last, 32 * k, 1) if k else last, before)
                for m in range(1, taps.shape[1] + 1):
                    start = start - taps[rows16, m - 1 : m] * pltpu.roll(before, m, 1)
                both.append(start)
            fixed.append(both)
        for when in range(1, 8):
            quad, k = when >> 2, when & 3
            first16 = jnp.concatenate([fixed[0][quad], fixed[1][quad]], axis=0)
            first16 = pltpu.roll(first16, (112 - 32 * k) % 128, 1)
            cols = slice(HALO + block_time * when, HALO + block_time * when + 128)
            old = white[at : at + 16, cols].astype(F32)
            white[at : at + 16, cols] = jnp.where(lane_iota((16, 128)) < 16, first16, old).astype(BF)

    tiles = 5
    for m in range(tiles):
        wide[64 * m : 64 * m + 64, :] = white[:, 1024 * m : 1024 * m + 1024 + HALO]
    for v in range(0, PH, 2):
        passed = jnp.dot(
            wide[...], b_ref[:, 128 * v : 128 * v + 256], preferred_element_type=F32
        ).astype(BF).astype(F32)
        for m in range(tiles):
            for e in range(2):
                f8[:, v + e, 128 * m : 128 * m + 128] = passed[
                    64 * m : 64 * m + 64, 128 * e : 128 * e + 128
                ]

    def align(c):
        move = moveouts_ref[c]
        move1 = jnp.right_shift(move, 3)
        move0 = jnp.bitwise_and(move, 7)
        turn = jnp.bitwise_and(8 - move0, 7)
        near = sub < 8 - move0
        whole = f8[c]
        x = [pltpu.roll(whole[:, 128 * i : 128 * i + 128], turn, 0) for i in range(5)]
        y0 = shift_left(x, move1, lane)
        y1 = shift_static(y0, 1, lane)
        y2 = shift_static(y1, 1, lane)
        a = [jnp.where(near, p, q) for p, q in zip(y0, y1)]
        nxt = [jnp.where(near, p, q) for p, q in zip(y1, y2)]
        a_ref[c] = jnp.concatenate(
            [jnp.concatenate([p, q], axis=0) for p, q in zip(a, nxt)], axis=1
        ).astype(BF)
        return jnp.concatenate(a, axis=1)

    def first(i, carry):
        for e in range(0, GROUP, 2):
            c = GROUP * i + e
            both = jnp.concatenate([align(c), align(c + 1)], axis=0)
            square = both * both
            high = square.astype(BF)
            at = pl.ds(pl.multiple_of(8 * c, 16), 16)
            high_ref[at, :] = high
            low_ref[at, :] = (square - high.astype(F32)).astype(BF)
            tail_rows[at, :] = pltpu.roll(both.astype(BF), 640 - 64, 1)[:, :rows]
        return carry

    lax.fori_loop(0, channels // GROUP, first, 0)

    for half in range(2):
        at = slice(256 * half, 256 * half + 384)
        sums[:, 256 * half : 256 * half + 256] = jnp.dot(
            high_ref[:, at], ones_ref[...], preferred_element_type=F32
        ) + jnp.dot(low_ref[:, at], ones_ref[...], preferred_element_type=F32)
    last = high_ref[:, 512:640].astype(F32) + low_ref[:, 512:640].astype(F32)
    last = jnp.sum(jnp.where(lane_iota((512, 128)) < 64, last, 0.0), axis=1, keepdims=True)
    sums[:, 512:640] = jnp.broadcast_to(last, (512, 128))

    def second(i, carry):
        for e in range(0, GROUP, 2):
            pair_scales = []
            for k in range(2):
                c = GROUP * i + e + k
                whole = sums[pl.ds(pl.multiple_of(8 * c, 8), 8), :]
                total = [whole[:, 128 * g : 128 * g + 128] for g in range(5)]
                after = shift_static(total, 1, lane)
                scales = []
                for g in range(groups):
                    suffix = total[g]
                    prefix = jnp.where(sub >= 1, pltpu.roll(after[g], 1, 0), 0.0)
                    for step in (1, 2, 4):
                        suffix = suffix + jnp.where(sub < 8 - step, pltpu.roll(suffix, 8 - step, 0), 0.0)
                        prefix = prefix + jnp.where(sub >= step, pltpu.roll(prefix, step, 0), 0.0)
                    scales.append(lax.rsqrt((suffix + prefix) / length + EPSILON))
                scales = jnp.concatenate(scales, axis=1)
                s_ref[c] = scales
                pair_scales.append(scales)
            at = pl.ds(pl.multiple_of(8 * (GROUP * i + e), 16), 16)
            tail = tail_rows[at, :].astype(F32)
            for t in range(1, PH):
                q_ref[t - 1, at, :] = jnp.concatenate(
                    [tail[8 * k : 8 * k + 8] * pair_scales[k][t : t + 1, :] for k in range(2)], axis=0
                ).astype(BF)
        return carry

    lax.fori_loop(0, channels // GROUP, second, 0)
    keep = lane_iota((16, 128))

    def build(c, h_ref):
        x = a_ref[c]
        for u in range(32):
            for g in range(groups):
                p, q = x[:, 128 * g : 128 * g + 128], x[:, 128 * g + 128 : 128 * g + 256]
                if u:
                    p = pltpu.roll(jnp.where(keep >= 2 * u, p, q), 128 - 2 * u, 1)
                h_ref[16 * u : 16 * u + 16, 128 * g : 128 * g + 128] = p

    def add_channel(h_ref, c):
        mask = m_ref[c].astype(F32)
        for nt in range(2):
            lanes = slice(256 * nt, 256 * nt + 256)
            for half in range(2):
                r = jnp.dot(
                    w_own[256 * half : 256 * half + 256, :], h_ref[:, lanes], preferred_element_type=F32
                )
                for t in range(4):
                    for g in range(2):
                        col = slice(256 * nt + 128 * g, 256 * nt + 128 * g + 128)
                        row = 4 * half + t
                        at = (slice(count * row, count * row + count), col)
                        part = r[count * t : count * t + count, 128 * g : 128 * g + 128]
                        acc[at] = acc[at] + part * (mask * s_ref[c, row : row + 1, col])

    acc[...] = jnp.zeros_like(acc)
    w_own[...] = w_ref[...]
    build(0, h0)

    def several(i, carry):
        for k in range(0, UNROLL, 2):
            c = UNROLL * i + k
            build(c + 1, h1)
            add_channel(h0, c)
            build(jnp.minimum(c + 2, channels - 1), h0)
            add_channel(h1, c + 1)
        return carry

    lax.fori_loop(0, channels // UNROLL, several, 0)

    wide_tmpl = tmpl_ref[...].astype(F32)
    power = jnp.mean(wide_tmpl * wide_tmpl, axis=1, keepdims=True)
    gain = 1.0 / (length * jnp.sqrt(power + EPSILON))
    for t in range(PH):
        at = slice(count * t, count * t + count)
        block = acc[at, :]
        if t:
            block = block + jnp.dot(tail_ref[t - 1], q_ref[t - 1], preferred_element_type=F32)
        turned[:, at] = (block * gain).T
    home = place_ref[1]
    for first_flip, ref in zip((0,) + FIRST, (keep_ref, *send_refs)):
        for p, second_flip in enumerate((0,) + SECOND):
            owner = jnp.bitwise_xor(home, first_flip ^ second_flip)
            part = turned[pl.ds(pl.multiple_of(32 * owner, 32), 32), :]
            ref[32 * p : 32 * p + 32, :] = part.astype(ref.dtype)


def gather_time(white):
    own = [white]
    for d in (1, 2, 3):
        own.append(lax.ppermute(white, "tm", [((q + 2 * d) % 8, q) for q in range(8)]))
    other = [lax.ppermute(p, "tm", [(q ^ 1, q) for q in range(8)]) for p in own]
    return own + other


def swap(value, flip):
    return lax.ppermute(value, "chan", [(i, i ^ flip) for i in range(lax.axis_size("chan"))])


def reduce_lags(kept, sent):
    total = kept
    for part, flip in zip([swap(p, f) for p, f in zip(sent, FIRST)], FIRST):
        total = total + part.astype(F32)
    narrow = total.astype(BF)
    rows = total.shape[0] // 4
    total = total[:rows]
    for k, flip in enumerate(SECOND):
        total = total + swap(narrow[rows * k + rows : rows * k + 2 * rows], flip).astype(F32)
    return total


def shards(raw_data, whiten_taps, band_taps, templates, channel_mask, moveouts):
    channels, block_time = raw_data.shape
    count, length = templates.shape
    white = pl.pallas_call(
        whiten_kernel,
        out_shape=jax.ShapeDtypeStruct((channels, block_time + 128), BF),
        in_specs=[VMEM] * 2,
        out_specs=VMEM,
        scratch_shapes=[pltpu.VMEM((channels, 128), F32)],
        compiler_params=pltpu.CompilerParams(vmem_limit_bytes=4 * 2**20),
    )(raw_data, whiten_taps.T)
    b, w = pl.pallas_call(
        setup_kernel,
        out_shape=[
            jax.ShapeDtypeStruct((1152, 1024), BF),
            jax.ShapeDtypeStruct((512, 512), BF),
        ],
        in_specs=[VMEM] * 2,
        out_specs=[VMEM] * 2,
        cost_estimate=pl.CostEstimate(flops=2**31, bytes_accessed=2**22, transcendentals=0),
        compiler_params=pltpu.CompilerParams(vmem_limit_bytes=8 * 2**20),
    )(band_taps.reshape(1, -1), templates)
    blocks = gather_time(white)
    place = jnp.stack([lax.axis_index("tm"), lax.axis_index("chan")]).astype(jnp.int32)
    kept, *sent = pl.pallas_call(
        stack_kernel,
        out_shape=[jax.ShapeDtypeStruct((128, PH * count), F32)]
        + [jax.ShapeDtypeStruct((128, PH * count), BF)] * 3,
        in_specs=[SMEM] * 2 + [VMEM] * 13,
        out_specs=[VMEM] * 4,
        scratch_shapes=[
            pltpu.VMEM((64, HALO + 5120), BF),
            pltpu.VMEM((8, 64, 128), F32),
            pltpu.VMEM((320, 1152), BF),
            pltpu.VMEM((64, 8, 640), F32),
            pltpu.VMEM((512, 512), BF),
            pltpu.VMEM((384, 256), BF),
            pltpu.VMEM((7, 64, 512), BF),
            pltpu.VMEM((64, 64, 128), BF),
            pltpu.VMEM((512, 512), BF),
            pltpu.VMEM((512, 512), BF),
            pltpu.VMEM((64, 16, 640), BF),
            pltpu.VMEM((64, 8, 512), F32),
            pltpu.VMEM((7, 512, 512), BF),
            pltpu.VMEM((512, 512), F32),
            pltpu.VMEM((512, 640), BF),
            pltpu.VMEM((512, 640), BF),
            pltpu.VMEM((512, 512), BF),
            pltpu.VMEM((512, 640), F32),
            pltpu.VMEM((512, 512), F32),
        ],
        cost_estimate=pl.CostEstimate(flops=2**34, bytes_accessed=2**23, transcendentals=0),
        compiler_params=pltpu.CompilerParams(vmem_limit_bytes=26 * 2**20),
    )(place, moveouts, *blocks, templates, channel_mask, whiten_taps.T, b, w)
    return reduce_lags(kept, sent).reshape(256, count)


def solution(mesh):
    in_specs = (P("chan", "tm"), P("chan", None), P(), P("tm", None), P("tm", "chan"), P("chan"))
    out_specs = P("chan", "tm")
    return jax.shard_map(shards, mesh=mesh, in_specs=in_specs, out_specs=out_specs, check_vma=False)
```
